256 devices in a mesh: dp: 64 (over y_lo, x, z), mp: 4 (over y_hi, core).
Axes of the slice: x: 4, y: 4 (y_hi: 2, y_lo: 2; y = y_hi * 2 + y_lo), z: 8, core: 2. Of those that a mesh axis runs over, the one named last changes fastest.
Arguments:
- img_feats: bfloat16 [131072, 1024], P('dp'), may hold values from -64 to 64
- txt_feats: bfloat16 [131072, 768], P('dp'), may hold values from -64 to 64
- img_weight: bfloat16 [1024, 768], P(None, 'mp'), may hold values from -1 to 1
- txt_weight: bfloat16 [768, 768], P(None, 'mp'), may hold values from -1 to 1
- row_lse: float32 [131072], P(('dp', 'mp')), may hold values from 10 to 16
- col_lse: float32 [131072], P('dp'), may hold values from 10 to 16
- labels: int32 [64, 2048], P('dp'), may hold values from 0 to 2047, as said below
Outputs:
- img_weight_grad: float32 [1024, 768], P(None, 'mp')
- txt_grad: float32 [131072, 768], P('dp', 'mp')
The draws below stay inside these ranges and needn't reach their ends.
Inputs may be any that keep to these rules, and one draw needn't show every extreme that they name: Each row of labels is a permutation of 0 to 2047.
All inputs are finite; a program needn't handle non-finite values.
Results may differ from the reference program's by a relative error of at most 0.004.
Values may be sent and summed in bfloat16 or wider, within the bound.
No kernel may reach another device: no remote copies, remote signals or barrier semaphores. Data moves between devices by JAX's collectives and lax.ppermute only.
A program may use at most 128 MiB of HBM per device.

```python
import math
import jax
import jax.numpy as jnp
from jax import lax

DI = 1024
DT = 768
E = 768
PAIRS_DP = 2048
STEPS = 2
PAIRS = 131072
N_DP = 64


shared_part = 0.7


head_align = 0.975


def pair_labels(key):
    shard_count = PAIRS // PAIRS_DP
    keys = jax.random.split(jax.random.fold_in(key, 11), shard_count)
    orders = jax.vmap(lambda single: jax.random.permutation(single, PAIRS_DP))(keys)
    return orders.astype(jnp.int32)


def pair_latents(key):
    shard_count = PAIRS // PAIRS_DP
    cluster_count = max(PAIRS_DP // 64, 1)
    cluster = jax.random.randint(jax.random.fold_in(key, 12), (shard_count, PAIRS_DP), 0, cluster_count)
    centres = jax.random.normal(jax.random.fold_in(key, 13), (shard_count, cluster_count, DT), jnp.float32)
    own_noise = jax.random.normal(jax.random.fold_in(key, 14), (shard_count, PAIRS_DP, DT), jnp.float32)
    following = jnp.roll(centres, -1, axis=0)
    select = jax.vmap(lambda lookup, position: lookup[position])
    text_latent = math.sqrt(shared_part) * math.sqrt(0.5) * (select(centres, cluster) + select(following, cluster))
    text_latent = text_latent + math.sqrt(1.0 - shared_part) * own_noise
    orders = pair_labels(key)
    matched_cluster = select(cluster, orders)
    matched_noise = select(own_noise, orders)
    image_latent = math.sqrt(shared_part) * select(centres, matched_cluster) + math.sqrt(1.0 - shared_part) * matched_noise
    return (image_latent.reshape(PAIRS, DT), text_latent.reshape(PAIRS, DT))


def mix_features(latent, noise, spread, key):
    strength = jax.random.uniform(jax.random.fold_in(key, 4), (latent.shape[0], 1), jnp.float32, 0.9, 1.0)
    leading = strength * latent + jnp.sqrt(1.0 - strength * strength) * noise[:, :DT]
    whole = jnp.concatenate([leading, noise[:, DT:]], axis=1)
    return jnp.clip(spread * whole, -64.0, 64.0).astype(jnp.bfloat16)


def head_common(key):
    return jnp.clip(jax.random.normal(jax.random.fold_in(key, 21), (DT, E), jnp.float32), -5.0, 5.0)


def draw_img_feats(key, part):
    image_latent, text_latent = pair_latents(key)
    key = jax.random.fold_in(key, 3)
    noise = jnp.clip(jax.random.normal(jax.random.fold_in(key, 1), (PAIRS, DI), jnp.float32), -5.0, 5.0)
    spread = jnp.exp(jax.random.uniform(jax.random.fold_in(key, 2), (PAIRS, 1), jnp.float32, 0.0, math.log(3.0)))
    return mix_features(image_latent, noise, spread, key)


def draw_txt_feats(key, part):
    image_latent, text_latent = pair_latents(key)
    key = jax.random.fold_in(key, 4)
    noise = jnp.clip(jax.random.normal(jax.random.fold_in(key, 1), (PAIRS, DT), jnp.float32), -5.0, 5.0)
    spread = jnp.exp(jax.random.uniform(jax.random.fold_in(key, 2), (PAIRS, 1), jnp.float32, 0.0, math.log(3.0)))
    return mix_features(text_latent, noise, spread, key)


def draw_img_weight(key, part):
    common = head_common(key)
    key = jax.random.fold_in(key, 5)
    noise = jnp.clip(jax.random.normal(key, (DI, E), jnp.float32), -5.0, 5.0)
    upper = head_align * common + math.sqrt(1.0 - head_align * head_align) * noise[:DT]
    lower = 0.3 * noise[DT:]
    return (jnp.concatenate([upper, lower], axis=0) / math.sqrt(DT)).astype(jnp.bfloat16)


def draw_txt_weight(key, part):
    common = head_common(key)
    key = jax.random.fold_in(key, 6)
    noise = jnp.clip(jax.random.normal(key, (DT, E), jnp.float32), -5.0, 5.0)
    mixed = head_align * common + math.sqrt(1.0 - head_align * head_align) * noise
    return (mixed / math.sqrt(DT)).astype(jnp.bfloat16)


def draw_row_lse(key, part):
    key = jax.random.fold_in(key, 7)
    jitter = jax.random.uniform(key, (PAIRS,), jnp.float32, -1.0, 1.0)
    return (jnp.log(jnp.float32(PAIRS) + 80000.0) + jitter).astype(jnp.float32)


def draw_col_lse(key, part):
    key = jax.random.fold_in(key, 8)
    jitter = jax.random.uniform(key, (PAIRS,), jnp.float32, -1.0, 1.0)
    return (jnp.log(jnp.float32(PAIRS) + 80000.0) + jitter).astype(jnp.float32)


def draw_labels(key, part):
    return pair_labels(key)


def setup_inputs(seed: int = 0) -> dict:
    streams_of = jax.random.split(jax.random.key(seed), 8)
    return {
        "img_feats": draw_img_feats(jax.random.fold_in(streams_of[7], 71), 0),
        "txt_feats": draw_txt_feats(jax.random.fold_in(streams_of[7], 71), 0),
        "img_weight": draw_img_weight(jax.random.fold_in(streams_of[7], 71), 0),
        "txt_weight": draw_txt_weight(jax.random.fold_in(streams_of[7], 71), 0),
        "row_lse": draw_row_lse(jax.random.fold_in(streams_of[7], 71), 0),
        "col_lse": draw_col_lse(jax.random.fold_in(streams_of[7], 71), 0),
        "labels": draw_labels(jax.random.fold_in(streams_of[7], 71), 0),
    }


scale_logit = 1.0 / 0.07
loss_weight = 0.25
epsilon = 1e-06

def normalize(raw):
    length = jnp.sqrt(lax.optimization_barrier(jnp.sum(raw * raw, -1, keepdims=True)) + epsilon)
    return (raw / length, length)

def reference(img_feats, txt_feats, img_weight, txt_weight, row_lse, col_lse, labels):
    img_raw = jnp.dot(img_feats, img_weight, preferred_element_type=jnp.float32)
    img_unit, img_len = normalize(img_raw)
    img_emb = img_unit.astype(jnp.bfloat16)
    txt_unit, txt_len = normalize(jnp.dot(txt_feats, txt_weight, preferred_element_type=jnp.float32))
    txt_emb = txt_unit.astype(jnp.bfloat16)
    width = img_emb.shape[1]
    images = img_emb.reshape(N_DP, PAIRS_DP, width)
    texts = txt_emb.reshape(N_DP, PAIRS_DP, width)
    row_stat = row_lse.reshape(N_DP, PAIRS_DP)
    col_stat = col_lse.reshape(N_DP, PAIRS_DP)

    def visit(shard_imgs, shard_rows, tile_txt, tile_cols, target):
        scores = scale_logit * jnp.dot(shard_imgs, tile_txt.T, preferred_element_type=jnp.float32)
        grads = (jnp.exp(scores - shard_rows[:, None]) + jnp.exp(scores - tile_cols[None, :]) - 2.0 * target) * loss_weight
        grads = grads.astype(jnp.bfloat16)
        img_part = scale_logit * jnp.dot(grads, tile_txt, preferred_element_type=jnp.float32)
        txt_part = scale_logit * jnp.dot(grads.T, shard_imgs, preferred_element_type=jnp.float32)
        return (img_part, txt_part)

    def per_shard(index):
        shard_imgs = images[index]
        shard_rows = row_stat[index]
        target = (labels[index][:, None] == jnp.arange(PAIRS_DP, dtype=jnp.int32)[None, :]).astype(jnp.float32)
        img_total = jnp.zeros((PAIRS_DP, width), jnp.float32)
        txt_parts = []
        for visit_index in range(STEPS):
            other = (index - visit_index) % N_DP
            mask = target if visit_index == 0 else jnp.zeros_like(target)
            img_part, txt_part = visit(shard_imgs, shard_rows, texts[other], col_stat[other], mask)
            img_total = img_total + img_part
            txt_parts.append(txt_part)
        return (img_total, jnp.stack(txt_parts))
    img_grad, txt_parts = lax.map(per_shard, jnp.arange(N_DP, dtype=jnp.int32))
    txt_grad = jnp.zeros((N_DP, PAIRS_DP, width), jnp.float32)
    for visit_index in range(STEPS):
        txt_grad = txt_grad + jnp.roll(txt_parts[:, visit_index], STEPS - 1 - visit_index, axis=0)
    img_grad = img_grad.reshape(N_DP * PAIRS_DP, width)
    d_raw = ((img_grad - img_unit * lax.optimization_barrier(jnp.sum(img_unit * img_grad, -1, keepdims=True))) / img_len).astype(jnp.bfloat16)
    weight_grad = jnp.dot(img_feats.T, d_raw, preferred_element_type=jnp.float32)
    return (weight_grad, txt_grad.reshape(N_DP * PAIRS_DP, width))
```

```python
import functools
import math

import jax
import jax.numpy as jnp
from jax import lax
from jax.experimental import pallas as pl
from jax.experimental.pallas import tpu as pltpu
from jax.sharding import Mesh, PartitionSpec as P

scale_logit = 1.0 / 0.07
loss_weight = 0.25
epsilon = 1e-06
exp_scale = scale_logit * math.log2(math.e)

AXES = ("yl", "x", "z", "yh", "core")
DP = ("yl", "x", "z")
MP = ("yh", "core")
BF = jnp.bfloat16
F32 = jnp.float32
VMEM_LIMIT = 56 * 1024 * 1024

NT = (((1,), (1,)), ((), ()))
NN = (((1,), (0,)), ((), ()))


def dot(a, b, dims):
    return lax.dot_general(a, b, dims, preferred_element_type=F32)


def routes(sizes, move):
    n_yl, n_x, n_z, n_yh, n_core = sizes

    def flat(p):
        yl, x, z, yh, core = p
        return (((yl * n_x + x) * n_z + z) * n_yh + yh) * n_core + core

    pairs = []
    for yl in range(n_yl):
        for x in range(n_x):
            for z in range(n_z):
                for yh in range(n_yh):
                    for core in range(n_core):
                        p = (yl, x, z, yh, core)
                        pairs.append((flat(p), flat(move(*p))))
    return pairs


def whole(n):
    return [pl.BlockSpec(memory_space=pltpu.VMEM)] * n


def call(body, outs, n_in, scratch=(), flops=0, bytes_accessed=0, transcendentals=0):
    return pl.pallas_call(
        body,
        out_shape=outs,
        in_specs=whole(n_in),
        out_specs=[pl.BlockSpec(memory_space=pltpu.VMEM)] * len(outs),
        scratch_shapes=list(scratch),
        compiler_params=pltpu.CompilerParams(vmem_limit_bytes=VMEM_LIMIT),
        cost_estimate=pl.CostEstimate(
            flops=flops, bytes_accessed=bytes_accessed, transcendentals=transcendentals
        ),
    )


def project_texts(feats_ref, wt_ref, emb_ref, own_t_ref, first_row, block):
    rows = feats_ref.shape[0]
    for r in range(0, rows, block):
        raw = dot(feats_ref[r : r + block, :], wt_ref[...], NT)
        inv = lax.rsqrt(jnp.sum(raw * raw, -1, keepdims=True) + epsilon)
        unit = raw * inv
        emb_ref[first_row + r : first_row + r + block, :] = unit.astype(BF)
        turned = jnp.transpose(unit[:, 0:256])
        cols = own_t_ref.shape[0]
        own_t_ref[:, first_row + r : first_row + r + block] = turned[0:cols, :].astype(BF)


def gather_weight(parts, w_ref):
    cols = parts[0].shape[0]
    for i, part in enumerate(parts):
        w_ref[i * cols : (i + 1) * cols, :] = part[...]


def project_kernel(
    img_ref, txt_ref, wi0, wi1, wi2, wi3, wt0, wt1, wt2, wt3,
    img_emb_t, img_own_t, inv_ref, txt_emb, txt_own_t, wi_s, wt_s,
):
    gather_weight((wt0, wt1, wt2, wt3), wt_s)
    gather_weight((wi0, wi1, wi2, wi3), wi_s)
    project_texts(txt_ref, wt_s, txt_emb, txt_own_t, 0, 512)
    rows = img_ref.shape[0]
    cols = img_own_t.shape[0]
    for r in range(0, rows, 256):
        raw = dot(wi_s[...], img_ref[r : r + 256, :], NT)
        inv = lax.rsqrt(jnp.sum(raw * raw, 0, keepdims=True) + epsilon)
        unit = raw * inv
        img_emb_t[:, r : r + 256] = unit.astype(BF)
        img_own_t[:, r : r + 256] = unit[0:cols, :]
        inv_ref[:, r : r + 256] = inv


def score_tile(
    txt_emb, txt_own_t, img_emb_t, row_ref, col_ref, label_ref, visit, txt_chunk=512, img_chunk=256
):
    texts = txt_emb.shape[0]
    images = img_emb_t.shape[1]
    cols = txt_own_t.shape[0]
    for i in range(0, images, img_chunk):
        img_part = jnp.zeros((cols, img_chunk), F32)
        along = jnp.zeros((1, img_chunk), F32)
        er = loss_weight * jnp.exp(-row_ref[:, i : i + img_chunk])
        for t in range(0, texts, txt_chunk):
            raw = dot(txt_emb[t : t + txt_chunk, :], img_emb_t[:, i : i + img_chunk], NN)
            ec = col_ref[t : t + txt_chunk, 0:1]
            g = jnp.exp2(raw * exp_scale) * (er + ec)
            if label_ref is not None:
                place = lax.broadcasted_iota(jnp.int32, (txt_chunk, img_chunk), 0)
                hit = place == (label_ref[:, i : i + img_chunk] - t)
                g = g - jnp.where(hit, 2.0 * loss_weight, 0.0)
            g = g.astype(BF)
            along = along + jnp.sum(g.astype(F32) * raw, 0, keepdims=True)
            img_part = img_part + dot(txt_own_t[:, t : t + txt_chunk], g, NN)
            visit(i, t, g)
        yield i, img_part, along


def first_tile_kernel(
    txt_emb, txt_own_t, img_emb_t, row_ref, col_ref, label_ref, img_part_ref, along_ref, txt_part_ref, g_s
):
    def keep(i, t, g):
        g_s[t : t + g.shape[0], i : i + g.shape[1]] = g

    for i, img_part, along in score_tile(
        txt_emb, txt_own_t, img_emb_t, row_ref, col_ref, label_ref, keep
    ):
        img_part_ref[:, i : i + img_part.shape[1]] = img_part
        along_ref[:, i : i + along.shape[1]] = along
    cols = txt_own_t.shape[0]
    for t in range(0, txt_emb.shape[0], 256):
        txt_part_ref[:, t : t + 256] = (
            scale_logit * dot(img_emb_t[0:cols, :], g_s[t : t + 256, :], NT)
        ).astype(BF)


def second_tile_kernel(
    feats_a, feats_b, wt0, wt1, wt2, wt3, img_emb_t, img_own_t, inv_ref, row_ref, col_ref,
    img_part_ref, along_ref, img_feats,
    weight_ref, txt_part_ref, wt_s, txt_emb, txt_own_t, d_raw, g_s,
):
    gather_weight((wt0, wt1, wt2, wt3), wt_s)
    half = feats_a.shape[0]
    project_texts(feats_a, wt_s, txt_emb, txt_own_t, 0, 512)
    project_texts(feats_b, wt_s, txt_emb, txt_own_t, half, 512)

    def keep(i, t, g):
        g_s[t : t + g.shape[0], i : i + g.shape[1]] = g

    for i, img_part, along in score_tile(
        txt_emb, txt_own_t, img_emb_t, row_ref, col_ref, None, keep
    ):
        at = slice(i, i + img_part.shape[1])
        grad = img_part_ref[:, at] + img_part
        along = along_ref[:, at] + along
        d_raw[:, at] = ((grad - img_own_t[:, at] * along) * (scale_logit * inv_ref[:, at])).astype(BF)
    for k in range(0, img_feats.shape[1], 256):
        weight_ref[:, k : k + 256] = dot(d_raw[...], img_feats[:, k : k + 256], NN)
    cols = txt_own_t.shape[0]
    for t in range(0, txt_emb.shape[0], 256):
        txt_part_ref[:, t : t + 256] = scale_logit * dot(img_emb_t[0:cols, :], g_s[t : t + 256, :], NT)


def local(sizes, img_feats, txt_feats, img_weight, txt_weight, row_lse, col_lse, labels):
    n_yl, n_x, n_z, n_yh, n_core = sizes
    n_dp = n_yl * n_x * n_z
    pairs = img_feats.shape[0]
    cols = img_weight.shape[1]
    width = cols * n_yh * n_core
    img_in, txt_in = img_feats.shape[1], txt_feats.shape[1]
    core = lax.axis_index("core")
    yh = lax.axis_index("yh")

    across = routes(sizes, lambda yl, x, z, h, c: (1 - yl, x, z, 1 - h, c))
    swap = routes(sizes, lambda yl, x, z, h, c: (yl, x, z, h, 1 - c))
    peer = routes(sizes, lambda yl, x, z, h, c: (yl, x, z, 1 - h, c))

    def following(yl, x, z, h, c):
        d = ((yl * n_x + x) * n_z + z + 1) % n_dp
        return (d // (n_x * n_z), (d // n_z) % n_x, d % n_z, h, c)

    onward = routes(sizes, following)

    def send(a, route):
        return lax.ppermute(a, AXES, route)

    wi, wt = img_weight.T, txt_weight.T
    wt_far = send(wt, across)
    wi_far = send(wi, across)
    half = pairs // n_core
    mine = lax.dynamic_slice_in_dim(txt_feats, core * half, half, 0)
    feats_a = send(mine, onward)
    col_prev = send(col_lse, onward)
    row_far = send(row_lse, peer)
    wt_near, wi_near = send(wt, swap), send(wi, swap)
    row_near, row_far_near = send(row_lse, swap), send(row_far, swap)
    wt_far_near, wi_far_near = send(wt_far, swap), send(wi_far, swap)
    feats_b = send(feats_a, swap)

    def ordered(bit, own, other):
        first = jnp.where(bit == 0, own, other)
        second = jnp.where(bit == 0, other, own)
        return jnp.concatenate([first, second], 0)

    row_all = ordered(yh, ordered(core, row_lse, row_near), ordered(core, row_far, row_far_near))[None, :]
    prev_local = ordered(core, col_prev[:half], col_prev[half:])
    lanes = 128
    col_own = jnp.broadcast_to((loss_weight * jnp.exp(-col_lse))[:, None], (pairs, lanes))
    col_prev = jnp.broadcast_to((loss_weight * jnp.exp(-prev_local))[:, None], (pairs, lanes))

    wts = (wt, wt_near, wt_far, wt_far_near)
    wis = (wi, wi_near, wi_far, wi_far_near)
    shape = jax.ShapeDtypeStruct
    img_emb_t, img_own_t, inv, txt_emb, txt_own_t = call(
        project_kernel,
        [
            shape((width, pairs), BF),
            shape((cols, pairs), F32),
            shape((1, pairs), F32),
            shape((pairs, width), BF),
            shape((cols, pairs), BF),
        ],
        10,
        [pltpu.VMEM((width, img_in), BF), pltpu.VMEM((width, txt_in), BF)],
        flops=2 * pairs * width * (img_in + txt_in),
        bytes_accessed=2 * pairs * (img_in + txt_in + 3 * width),
    )(img_feats, txt_feats, *wis, *wts)

    tile_flops = 2 * pairs * pairs * (width + 2 * cols)
    img_part, along, txt_part = call(
        first_tile_kernel,
        [shape((cols, pairs), F32), shape((1, pairs), F32), shape((cols, pairs), BF)],
        6,
        [pltpu.VMEM((pairs, pairs), BF)],
        flops=tile_flops,
        bytes_accessed=4 * pairs * width * 2,
        transcendentals=pairs * pairs,
    )(txt_emb, txt_own_t, img_emb_t, row_all, col_own, labels)
    txt_carry = send(txt_part, onward)

    weight_part, txt_last = call(
        second_tile_kernel,
        [shape((cols, img_in), F32), shape((cols, pairs), F32)],
        14,
        [
            pltpu.VMEM((width, txt_in), BF),
            pltpu.VMEM((pairs, width), BF),
            pltpu.VMEM((cols, pairs), BF),
            pltpu.VMEM((cols, pairs), BF),
            pltpu.VMEM((pairs, pairs), BF),
        ],
        flops=tile_flops + 2 * pairs * width * txt_in,
        bytes_accessed=6 * pairs * width * 2,
        transcendentals=pairs * pairs,
    )(
        feats_a, feats_b, *wts, img_emb_t, img_own_t, inv, row_all, col_prev,
        img_part, along, img_feats,
    )
    txt_local = jnp.concatenate(
        [
            jnp.where(core == 0, txt_last[:, :half], txt_last[:, half:]),
            jnp.where(core == 0, txt_last[:, half:], txt_last[:, :half]),
        ],
        1,
    )
    txt_grad = (txt_local + txt_carry.astype(F32)).T

    rg = 8
    cg = n_dp // rg
    rb, cb = cols // rg, img_in // cg
    pieces = weight_part.astype(BF).reshape(rg, rb, cg, cb).transpose(0, 2, 1, 3).reshape(n_dp, rb, cb)
    got = lax.all_to_all(pieces, DP, 0, 0, tiled=True)
    total = jnp.sum(got.astype(F32), 0).astype(BF)
    spread = jnp.broadcast_to(total[None], (n_dp, rb, cb))
    back = lax.all_to_all(spread, DP, 0, 0, tiled=True)
    weight_grad = back.reshape(rg, cg, rb, cb).transpose(0, 2, 1, 3).reshape(cols, img_in).astype(F32).T
    return weight_grad, txt_grad


def solution(mesh):
    n_dp, n_mp = mesh.devices.shape
    sizes = (2, 4, n_dp // 8, 2, n_mp // 2)
    fine = Mesh(mesh.devices.reshape(sizes), AXES)
    placed = (
        P(DP, None),
        P(DP, None),
        P(None, MP),
        P(None, MP),
        P(DP + MP),
        P(DP),
        P(DP, None),
    )
    return jax.shard_map(
        functools.partial(local, sizes),
        mesh=fine,
        in_specs=placed,
        out_specs=(P(None, MP), P(DP, MP)),
        check_vma=False,
    )
```

```python
import functools
import math

import jax
import jax.numpy as jnp
from jax import lax
from jax.experimental import pallas as pl
from jax.experimental.pallas import tpu as pltpu
from jax.sharding import Mesh, PartitionSpec as P

scale_logit = 1.0 / 0.07
loss_weight = 0.25
epsilon = 1e-06
exp_scale = scale_logit * math.log2(math.e)

AXES = ("yl", "x", "z", "yh", "core")
DP = ("yl", "x", "z")
MP = ("yh", "core")
BF = jnp.bfloat16
F32 = jnp.float32
VMEM_LIMIT = 56 * 1024 * 1024
TXT_CHUNK, IMG_CHUNK = 512, 1024

NT = (((1,), (1,)), ((), ()))
NN = (((1,), (0,)), ((), ()))


def dot(a, b, dims):
    return lax.dot_general(a, b, dims, preferred_element_type=F32)


def routes(sizes, move):
    n_yl, n_x, n_z, n_yh, n_core = sizes

    def flat(p):
        yl, x, z, yh, core = p
        return (((yl * n_x + x) * n_z + z) * n_yh + yh) * n_core + core

    pairs = []
    for yl in range(n_yl):
        for x in range(n_x):
            for z in range(n_z):
                for yh in range(n_yh):
                    for core in range(n_core):
                        p = (yl, x, z, yh, core)
                        pairs.append((flat(p), flat(move(*p))))
    return pairs


VMEM = pl.BlockSpec(memory_space=pltpu.VMEM)
ANY = pl.BlockSpec(memory_space=pl.ANY)


def call(body, ins, outs, scratch, flops, bytes_accessed, transcendentals=0):
    return pl.pallas_call(
        body,
        out_shape=[shape for shape, _ in outs],
        in_specs=ins,
        out_specs=[spec for _, spec in outs],
        scratch_shapes=scratch,
        compiler_params=pltpu.CompilerParams(vmem_limit_bytes=VMEM_LIMIT),
        cost_estimate=pl.CostEstimate(
            flops=0, bytes_accessed=0, transcendentals=0
        ),
    )


def copies(pairs, sems):
    made = [pltpu.make_async_copy(a, b, sems.at[n]) for n, (a, b) in enumerate(pairs)]
    for c in made:
        c.start()
    return made


def near_kernel(
    img_hbm, txt_hbm, w0, w1, row_ref,
    img_raw, txt_raw, er_ref,
    img_s, txt_s, wi_s, wt_s, sems,
):
    txt_in, img_in = copies([(txt_hbm, txt_s), (img_hbm, img_s)], sems)
    er_ref[...] = loss_weight * jnp.exp(-row_ref[...])
    cols = w0.shape[0]
    depth = wi_s.shape[1]
    for n, w in enumerate((w0, w1)):
        wi_s[n * cols : (n + 1) * cols, :] = w[:, 0:depth]
        wt_s[n * cols : (n + 1) * cols, :] = w[:, depth:]
    pairs = img_s.shape[0]
    txt_in.wait()
    for r in range(0, pairs, 512):
        txt_raw[r : r + 512, :] = dot(txt_s[r : r + 512, :], wt_s[...], NT)
    img_in.wait()
    for r in range(0, pairs, 512):
        img_raw[:, r : r + 512] = dot(wi_s[...], img_s[r : r + 512, :], NT)


def stand(lse_ref, first, column_ref):
    for n in range(column_ref.shape[0] // 128):
        weight = loss_weight * jnp.exp(-lse_ref[pl.ds(first + n, 1), :])
        column_ref[n * 128 : (n + 1) * 128, :] = jnp.transpose(jnp.broadcast_to(weight, (128, 128)))


def score_tile(
    txt_emb, txt_own_t, img_emb_t, er_ref, ec_s, label_ref, g_s, finish, txt_chunk, img_chunk
):
    texts = txt_emb.shape[0]
    images = img_emb_t.shape[1]
    cols = txt_own_t.shape[0]
    for i in range(0, images, img_chunk):
        at = slice(i, i + img_chunk)
        img_part = jnp.zeros((cols, img_chunk), F32)
        along = jnp.zeros((1, img_chunk), F32)
        er = er_ref[:, at]
        for t in range(0, texts, txt_chunk):
            raw = dot(txt_emb[t : t + txt_chunk, :], img_emb_t[:, at], NN)
            g = jnp.exp2(raw * exp_scale) * (er + ec_s[t : t + txt_chunk, 0:1])
            if label_ref is not None:
                place = lax.broadcasted_iota(jnp.int32, (txt_chunk, img_chunk), 0)
                g = g - jnp.where(place == (label_ref[:, at] - t), 2.0 * loss_weight, 0.0)
            g = g.astype(BF)
            along = along + jnp.sum(g.astype(F32) * raw, 0, keepdims=True)
            img_part = img_part + dot(txt_own_t[:, t : t + txt_chunk], g, NN)
            g_s[t : t + txt_chunk, at] = g
        finish(at, img_part, along)


def text_part(g_s, img_emb_t, cols, out_ref):
    for t in range(0, g_s.shape[0], 256):
        out_ref[:, t : t + 256] = (
            scale_logit * dot(img_emb_t[0:cols, :], g_s[t : t + 256, :], NT)
        ).astype(out_ref.dtype)


def first_kernel(
    txt_hbm, txt_raw_hbm, img_hbm, img_raw_hbm, w0, w1, w2, w3, er_ref, col_ref, label_ref,
    img_emb_hbm, img_own_hbm, wt_hbm, inv_ref, img_part_ref, along_ref, txt_part_ref,
    txt_s, txt_raw, img_s, img_raw, wi_s, wt_s, txt_emb, txt_own_t, img_emb_t, img_own_t, ec_s, g_s,
    sems, out_sems,
):
    loads = copies(
        [(txt_hbm, txt_s), (txt_raw_hbm, txt_raw), (img_hbm, img_s), (img_raw_hbm, img_raw)], sems
    )
    cols = w0.shape[0]
    depth = wi_s.shape[1]
    for n, w in enumerate((w0, w1, w2, w3)):
        wt_s[n * cols : (n + 1) * cols, :] = w[:, depth:]
    for n, w in enumerate((w2, w3)):
        wi_s[n * cols : (n + 1) * cols, :] = w[:, 0:depth]
    stand(col_ref, 0, ec_s)
    save_wt = pltpu.make_async_copy(wt_s, wt_hbm, out_sems.at[0])
    save_wt.start()
    pairs = txt_s.shape[0]
    two = 2 * cols
    loads[0].wait()
    loads[1].wait()
    for r in range(0, pairs, 512):
        far = dot(txt_s[r : r + 512, :], wt_s[two:, :], NT)
        near = txt_raw[r : r + 512, :]
        total = jnp.sum(near * near, -1, keepdims=True) + jnp.sum(far * far, -1, keepdims=True)
        inv = lax.rsqrt(total + epsilon)
        near = near * inv
        txt_emb[r : r + 512, 0:two] = near.astype(BF)
        txt_emb[r : r + 512, two:] = (far * inv).astype(BF)
        txt_own_t[:, r : r + 512] = jnp.transpose(near[:, 0:256])[0:cols, :].astype(BF)
    loads[2].wait()
    loads[3].wait()
    for r in range(0, pairs, 512):
        at = slice(r, r + 512)
        far = dot(wi_s[...], img_s[at, :], NT)
        near = img_raw[:, at]
        total = jnp.sum(near * near, 0, keepdims=True) + jnp.sum(far * far, 0, keepdims=True)
        inv = lax.rsqrt(total + epsilon)
        near = near * inv
        img_emb_t[0:two, at] = near.astype(BF)
        img_emb_t[two:, at] = (far * inv).astype(BF)
        img_own_t[:, at] = near[0:cols, :]
        inv_ref[:, at] = inv
    saves = [
        pltpu.make_async_copy(img_emb_t, img_emb_hbm, out_sems.at[1]),
        pltpu.make_async_copy(img_own_t, img_own_hbm, out_sems.at[2]),
    ]
    for c in saves:
        c.start()

    def finish(at, img_part, along):
        img_part_ref[:, at] = img_part
        along_ref[:, at] = along

    score_tile(
        txt_emb, txt_own_t, img_emb_t, er_ref, ec_s, label_ref, g_s, finish, TXT_CHUNK, IMG_CHUNK
    )
    text_part(g_s, img_emb_t, cols, txt_part_ref)
    save_wt.wait()
    for c in saves:
        c.wait()


def project_texts(feats_ref, wt_ref, emb_ref, own_t_ref):
    cols = own_t_ref.shape[0]
    for r in range(0, emb_ref.shape[0], 512):
        raw = dot(feats_ref[r : r + 512, :], wt_ref[...], NT)
        unit = raw * lax.rsqrt(jnp.sum(raw * raw, -1, keepdims=True) + epsilon)
        emb_ref[r : r + 512, :] = unit.astype(BF)
        own_t_ref[:, r : r + 512] = jnp.transpose(unit[:, 0:256])[0:cols, :].astype(BF)


def stand_half(feats, place, lse_s, ec_s):
    half = ec_s.shape[0]
    parts = [feats[half:, n * 128 : (n + 1) * 128].astype(F32) for n in range(3)]
    lse_s[...] = (parts[0] + parts[1]) + parts[2]
    stand(lse_s, place * (half // 128), ec_s)


def second_kernel(
    feats, wt, img_emb_hbm, er_ref, img_part_hbm, along_in,
    img_part_ref, along_ref, txt_part_ref,
    img_emb_t, img_part_s, txt_emb, txt_own_t, lse_s, ec_s, g_s, sems,
):
    loads = copies([(img_emb_hbm, img_emb_t), (img_part_hbm, img_part_s)], sems)
    stand_half(feats, lax.axis_index("core"), lse_s, ec_s)
    project_texts(feats, wt, txt_emb, txt_own_t)
    for c in loads:
        c.wait()

    def finish(at, img_part, along):
        img_part_ref[:, at] = img_part_s[:, at] + img_part
        along_ref[:, at] = along_in[:, at] + along

    score_tile(
        txt_emb, txt_own_t, img_emb_t, er_ref, ec_s, None, g_s, finish, TXT_CHUNK, IMG_CHUNK
    )
    text_part(g_s, img_emb_t, txt_own_t.shape[0], txt_part_ref)


def last_kernel(
    feats, wt, img_emb_hbm, er_ref, img_part_hbm, along_in, img_own_hbm, inv_ref, img_hbm,
    pieces_ref, txt_part_ref,
    img_emb_t, img_part_s, img_own_t, img_s, txt_emb, txt_own_t, lse_s, ec_s, g_s, d_raw, sems,
):
    loads = copies(
        [
            (img_emb_hbm, img_emb_t), (img_part_hbm, img_part_s),
            (img_own_hbm, img_own_t), (img_hbm, img_s),
        ],
        sems,
    )
    stand_half(feats, 1 - lax.axis_index("core"), lse_s, ec_s)
    project_texts(feats, wt, txt_emb, txt_own_t)
    for c in loads:
        c.wait()

    def finish(at, img_part, along):
        grad = img_part_s[:, at] + img_part
        toward = along_in[:, at] + along
        d_raw[:, at] = (
            (grad - img_own_t[:, at] * toward) * (scale_logit * inv_ref[:, at])
        ).astype(BF)

    score_tile(
        txt_emb, txt_own_t, img_emb_t, er_ref, ec_s, None, g_s, finish, TXT_CHUNK, IMG_CHUNK
    )
    n_pieces, rb, cb = pieces_ref.shape
    across = img_s.shape[1] // cb
    for k in range(0, img_s.shape[1], 256):
        part = dot(d_raw[...], img_s[:, k : k + 256], NN)
        for r in range(n_pieces // across):
            for c in range(256 // cb):
                pieces_ref[r * across + k // cb + c] = part[
                    r * rb : (r + 1) * rb, c * cb : (c + 1) * cb
                ].astype(BF)
    text_part(g_s, img_emb_t, txt_own_t.shape[0], txt_part_ref)


def text_total_kernel(part_a, part_b, carry, out_ref):
    half = part_a.shape[1]
    core = lax.axis_index("core")
    for place, part in ((core, part_a), (1 - core, part_b)):
        at = pl.ds(pl.multiple_of(place * half, half), half)
        out_ref[:, at] = part[...] + carry[:, at].astype(F32)


def local(sizes, img_feats, txt_feats, img_weight, txt_weight, row_lse, col_lse, labels):
    n_yl, n_x, n_z, n_yh, n_core = sizes
    n_dp = n_yl * n_x * n_z
    pairs = img_feats.shape[0]
    cols = img_weight.shape[1]
    width = cols * n_yh * n_core
    img_in, txt_in = img_feats.shape[1], txt_feats.shape[1]
    core = lax.axis_index("core")
    yh = lax.axis_index("yh")

    across = routes(sizes, lambda yl, x, z, h, c: (1 - yl, x, z, 1 - h, c))
    swap = routes(sizes, lambda yl, x, z, h, c: (yl, x, z, h, 1 - c))
    peer = routes(sizes, lambda yl, x, z, h, c: (yl, x, z, 1 - h, c))

    cross = routes(sizes, lambda yl, x, z, h, c: (yl, x, z, 1 - h, 1 - c))

    def following(yl, x, z, h, c):
        d = ((yl * n_x + x) * n_z + z + 1) % n_dp
        return (d // (n_x * n_z), (d // n_z) % n_x, d % n_z, h, c)

    onward = routes(sizes, following)

    def send(a, route):
        return lax.ppermute(a, AXES, route)

    def ordered(bit, own, other):
        first = jnp.where(bit == 0, own, other)
        second = jnp.where(bit == 0, other, own)
        return jnp.concatenate([first, second], 1)

    shape = jax.ShapeDtypeStruct
    half = pairs // n_core
    w_own = jnp.concatenate([img_weight.T, txt_weight.T], 1)
    w_far = send(w_own, across)
    w_near = send(w_own, swap)
    w_far_near = send(w_far, swap)
    lse = col_lse.reshape(pairs // 128, 128)
    high = lax.reduce_precision(lse, 8, 7)
    middle = lax.reduce_precision(lse - high, 8, 7)
    low = (lse - high) - middle
    lse_rows = jnp.concatenate([high, middle, low], 1).astype(BF)
    lse_rows = jnp.pad(lse_rows, ((0, 0), (0, txt_in - 3 * 128)))
    mine = lax.dynamic_slice_in_dim(txt_feats, core * half, half, 0)
    feats_a = send(jnp.concatenate([mine, lse_rows], 0), onward)

    img_raw, txt_raw, er_own = call(
        near_kernel,
        [ANY, ANY, VMEM, VMEM, VMEM],
        [
            (shape((2 * cols, pairs), F32), VMEM),
            (shape((pairs, 2 * cols), F32), VMEM),
            (shape((1, row_lse.shape[0]), F32), VMEM),
        ],
        [
            pltpu.VMEM((pairs, img_in), BF),
            pltpu.VMEM((pairs, txt_in), BF),
            pltpu.VMEM((2 * cols, img_in), BF),
            pltpu.VMEM((2 * cols, txt_in), BF),
            pltpu.SemaphoreType.DMA((2,)),
        ],
        2 * pairs * 2 * cols * (img_in + txt_in),
        2 * pairs * (img_in + txt_in + 2 * width),
    )(img_feats, txt_feats, w_own, w_near, row_lse[None, :])
    er_near = send(er_own, swap)
    er_far = send(er_own, peer)
    er_far_near = send(er_own, cross)
    er = ordered(yh, ordered(core, er_own, er_near), ordered(core, er_far, er_far_near))

    tile_flops = 2 * pairs * pairs * (width + 2 * cols)
    img_emb_t, img_own_t, wt, inv, img_part, along, txt_part = call(
        first_kernel,
        [ANY] * 4 + [VMEM] * 7,
        [
            (shape((width, pairs), BF), ANY),
            (shape((cols, pairs), F32), ANY),
            (shape((width, txt_in), BF), ANY),
            (shape((1, pairs), F32), VMEM),
            (shape((cols, pairs), F32), VMEM),
            (shape((1, pairs), F32), VMEM),
            (shape((cols, pairs), BF), VMEM),
        ],
        [
            pltpu.VMEM((pairs, txt_in), BF),
            pltpu.VMEM((pairs, 2 * cols), F32),
            pltpu.VMEM((pairs, img_in), BF),
            pltpu.VMEM((2 * cols, pairs), F32),
            pltpu.VMEM((2 * cols, img_in), BF),
            pltpu.VMEM((width, txt_in), BF),
            pltpu.VMEM((pairs, width), BF),
            pltpu.VMEM((cols, pairs), BF),
            pltpu.VMEM((width, pairs), BF),
            pltpu.VMEM((cols, pairs), F32),
            pltpu.VMEM((pairs, 128), F32),
            pltpu.VMEM((pairs, pairs), BF),
            pltpu.SemaphoreType.DMA((4,)),
            pltpu.SemaphoreType.DMA((3,)),
        ],
        tile_flops,
        4 * pairs * width * 2,
        pairs * pairs,
    )(
        txt_feats, txt_raw, img_feats, img_raw, w_own, w_near, w_far, w_far_near, er, lse, labels
    )
    txt_carry = send(txt_part, onward)
    feats_a, along = lax.optimization_barrier((feats_a, along))
    feats_b = send(feats_a, swap)

    half_scratch = [
        pltpu.VMEM((half, width), BF),
        pltpu.VMEM((cols, half), BF),
        pltpu.VMEM((pairs // 128, 128), F32),
        pltpu.VMEM((half, 128), F32),
        pltpu.VMEM((half, pairs), BF),
    ]
    img_part, along, txt_a = call(
        second_kernel,
        [VMEM, VMEM, ANY, VMEM, ANY, VMEM],
        [
            (shape((cols, pairs), F32), VMEM),
            (shape((1, pairs), F32), VMEM),
            (shape((cols, half), F32), VMEM),
        ],
        [pltpu.VMEM((width, pairs), BF), pltpu.VMEM((cols, pairs), F32)]
        + half_scratch
        + [pltpu.SemaphoreType.DMA((2,))],
        tile_flops // 2,
        2 * pairs * width * 2,
        pairs * half,
    )(feats_a, wt, img_emb_t, er, img_part, along)
    pieces, txt_b = call(
        last_kernel,
        [VMEM, VMEM, ANY, VMEM, ANY, VMEM, ANY, VMEM, ANY],
        [(shape((n_dp, cols * img_in // (128 * n_dp), 128), BF), VMEM), (shape((cols, half), F32), VMEM)],
        [
            pltpu.VMEM((width, pairs), BF),
            pltpu.VMEM((cols, pairs), F32),
            pltpu.VMEM((cols, pairs), F32),
            pltpu.VMEM((pairs, img_in), BF),
        ]
        + half_scratch
        + [pltpu.VMEM((cols, pairs), BF), pltpu.SemaphoreType.DMA((4,))],
        tile_flops // 2,
        2 * pairs * width * 2,
        pairs * half,
    )(feats_b, wt, img_emb_t, er, img_part, along, img_own_t, inv, img_feats)

    pieces, txt_carry = lax.optimization_barrier((pieces, txt_carry))
    got = lax.all_to_all(pieces, DP, 0, 0, tiled=True)
    total = jnp.sum(got.astype(F32), 0).astype(BF)
    spread = jnp.broadcast_to(total[None], pieces.shape)
    back = lax.all_to_all(spread, DP, 0, 0, tiled=True)
    (txt_total,) = call(
        text_total_kernel,
        [VMEM] * 3,
        [(shape((cols, pairs), F32), VMEM)],
        [],
        0,
        10 * cols * pairs,
    )(txt_a, txt_b, txt_carry)
    across_pieces = img_in // 128
    tiles = back.reshape(n_dp // across_pieces, across_pieces, pieces.shape[1], 128)
    weight_total = tiles.transpose(0, 2, 1, 3).reshape(cols, img_in).astype(F32)
    return weight_total.T, txt_total.T


def solution(mesh):
    n_dp, n_mp = mesh.devices.shape
    sizes = (2, 4, n_dp // 8, 2, n_mp // 2)
    fine = Mesh(mesh.devices.reshape(sizes), AXES)
    placed = (
        P(DP, None),
        P(DP, None),
        P(None, MP),
        P(None, MP),
        P(DP + MP),
        P(DP),
        P(DP, None),
    )
    return jax.shard_map(
        functools.partial(local, sizes),
        mesh=fine,
        in_specs=placed,
        out_specs=(P(None, MP), P(DP, MP)),
        check_vma=False,
    )
```

```python
import functools
import math

import jax
import jax.numpy as jnp
from jax import lax
from jax.experimental import pallas as pl
from jax.experimental.pallas import tpu as pltpu
from jax.sharding import Mesh, PartitionSpec as P

scale_logit = 1.0 / 0.07
loss_weight = 0.25
epsilon = 1e-06
exp_scale = scale_logit * math.log2(math.e)

AXES = ("yl", "x", "z", "yh", "core")
DP = ("yl", "x", "z")
MP = ("yh", "core")
BF = jnp.bfloat16
F32 = jnp.float32
VMEM_LIMIT = 56 * 1024 * 1024
TXT_CHUNK, IMG_CHUNK = 512, 256

NT = (((1,), (1,)), ((), ()))
NN = (((1,), (0,)), ((), ()))


def dot(a, b, dims):
    return lax.dot_general(a, b, dims, preferred_element_type=F32)


def routes(sizes, move):
    n_yl, n_x, n_z, n_yh, n_core = sizes

    def flat(p):
        yl, x, z, yh, core = p
        return (((yl * n_x + x) * n_z + z) * n_yh + yh) * n_core + core

    pairs = []
    for yl in range(n_yl):
        for x in range(n_x):
            for z in range(n_z):
                for yh in range(n_yh):
                    for core in range(n_core):
                        p = (yl, x, z, yh, core)
                        pairs.append((flat(p), flat(move(*p))))
    return pairs


VMEM = pl.BlockSpec(memory_space=pltpu.VMEM)
ANY = pl.BlockSpec(memory_space=pl.ANY)


def call(body, ins, outs, scratch, flops, bytes_accessed, transcendentals=0):
    return pl.pallas_call(
        body,
        out_shape=[shape for shape, _ in outs],
        in_specs=ins,
        out_specs=[spec for _, spec in outs],
        scratch_shapes=scratch,
        compiler_params=pltpu.CompilerParams(vmem_limit_bytes=VMEM_LIMIT),
        cost_estimate=pl.CostEstimate(
            flops=0, bytes_accessed=0, transcendentals=0
        ),
    )


def copies(pairs, sems):
    made = [pltpu.make_async_copy(a, b, sems.at[n]) for n, (a, b) in enumerate(pairs)]
    for c in made:
        c.start()
    return made


def parcel_kernel(txt_hbm, lse_ref, wi_hbm, wt_hbm, out_ref, w_ref, sems):
    rows = out_ref.shape[0] - lse_ref.shape[0]
    depth = wi_hbm.shape[1]
    first = pl.multiple_of(lax.axis_index("core") * rows, rows)
    loads = copies(
        [
            (wi_hbm, w_ref.at[:, pl.ds(0, depth)]),
            (wt_hbm, w_ref.at[:, pl.ds(depth, wt_hbm.shape[1])]),
            (txt_hbm.at[pl.ds(first, rows), :], out_ref.at[pl.ds(0, rows), :]),
        ],
        sems,
    )
    lse = lse_ref[...]
    high = lse.astype(BF)
    rest = lse - high.astype(F32)
    middle = rest.astype(BF)
    low = (rest - middle.astype(F32)).astype(BF)
    for n, part in enumerate((high, middle, low)):
        out_ref[rows:, n * 128 : (n + 1) * 128] = part
    out_ref[rows:, 384:] = jnp.zeros((lse.shape[0], out_ref.shape[1] - 384), BF)
    for c in loads:
        c.wait()


def row_blocks(pairs):
    return [pl.ds(r, pairs // 4) for r in range(0, pairs, pairs // 4)]


def near_kernel(
    img_hbm, txt_hbm, w0, w1, row_ref,
    img_raw, txt_raw, er_ref,
    img_s, txt_s, wi_s, wt_s, sems,
):
    pairs, depth = img_s.shape
    block = pairs // 4
    blocks = row_blocks(pairs)
    loads = copies(
        [(txt_hbm.at[b, :], txt_s.at[b, :]) for b in blocks]
        + [(img_hbm.at[b, :], img_s.at[b, :]) for b in blocks],
        sems,
    )
    er_ref[...] = loss_weight * jnp.exp(-row_ref[...])
    cols = w0.shape[0]
    for n, w in enumerate((w0, w1)):
        wi_s[n * cols : (n + 1) * cols, :] = w[:, 0:depth]
        wt_s[n * cols : (n + 1) * cols, :] = w[:, depth:]
    for n in range(4):
        at = slice(n * block, (n + 1) * block)
        loads[n].wait()
        txt_raw[at, :] = dot(txt_s[at, :], wt_s[...], NT)
    for n in range(4):
        at = slice(n * block, (n + 1) * block)
        loads[4 + n].wait()
        img_raw[:, at] = dot(wi_s[...], img_s[at, :], NT)


def stand(lse_ref, first, column_ref):
    for n in range(column_ref.shape[0] // 128):
        weight = loss_weight * jnp.exp(-lse_ref[pl.ds(first + n, 1), :])
        column_ref[n * 128 : (n + 1) * 128, :] = jnp.transpose(jnp.broadcast_to(weight, (128, 128)))


def score_tile(txt_emb, txt_own_t, img_emb_t, er_ref, ec_s, label_ref, g_s, finish):
    texts = txt_emb.shape[0]
    for i in range(0, img_emb_t.shape[1], IMG_CHUNK):
        at = slice(i, i + IMG_CHUNK)
        along = jnp.zeros((1, IMG_CHUNK), F32)
        er = er_ref[:, at]
        for t in range(0, texts, TXT_CHUNK):
            raw = dot(txt_emb[t : t + TXT_CHUNK, :], img_emb_t[:, at], NN)
            g = jnp.exp2(raw * exp_scale) * (er + ec_s[t : t + TXT_CHUNK, 0:1])
            if label_ref is not None:
                place = lax.broadcasted_iota(jnp.int32, (TXT_CHUNK, IMG_CHUNK), 0)
                g = g - jnp.where(place == (label_ref[:, at] - t), 2.0 * loss_weight, 0.0)
            g = g.astype(BF)
            along = along + jnp.sum(g.astype(F32) * raw, 0, keepdims=True)
            g_s[t : t + TXT_CHUNK, at] = g
        finish(at, dot(txt_own_t[...], g_s[:, at], NN), along)


def text_part(g_s, img_emb_t, cols, out_ref):
    for t in range(0, g_s.shape[0], 256):
        out_ref[:, t : t + 256] = (
            scale_logit * dot(img_emb_t[0:cols, :], g_s[t : t + 256, :], NT)
        ).astype(out_ref.dtype)


def first_kernel(
    txt_hbm, txt_raw_hbm, img_hbm, img_raw_hbm, w0, w1, w2, w3, er_ref, col_ref, label_ref,
    img_emb_hbm, img_own_hbm, wt_hbm, inv_ref, img_part_ref, along_ref, txt_part_ref,
    txt_s, txt_raw, img_s, img_raw, wi_s, wt_s, txt_emb, txt_own_t, img_emb_t, img_own_t, ec_s, g_s,
    sems, out_sems,
):
    pairs = txt_s.shape[0]
    block = pairs // 4
    blocks = row_blocks(pairs)
    moves = []
    for b in blocks:
        moves += [(txt_hbm.at[b, :], txt_s.at[b, :]), (txt_raw_hbm.at[b, :], txt_raw.at[b, :])]
    for b in blocks:
        moves += [(img_hbm.at[b, :], img_s.at[b, :]), (img_raw_hbm.at[:, b], img_raw.at[:, b])]
    loads = copies(moves, sems)
    cols = w0.shape[0]
    depth = wi_s.shape[1]
    for n, w in enumerate((w0, w1, w2, w3)):
        wt_s[n * cols : (n + 1) * cols, :] = w[:, depth:]
    for n, w in enumerate((w2, w3)):
        wi_s[n * cols : (n + 1) * cols, :] = w[:, 0:depth]
    stand(col_ref, 0, ec_s)
    save_wt = pltpu.make_async_copy(wt_s, wt_hbm, out_sems.at[0])
    save_wt.start()
    two = 2 * cols
    for n, r in enumerate(range(0, pairs, block)):
        loads[2 * n].wait()
        loads[2 * n + 1].wait()
        far = dot(txt_s[r : r + block, :], wt_s[two:, :], NT)
        near = txt_raw[r : r + block, :]
        total = jnp.sum(near * near, -1, keepdims=True) + jnp.sum(far * far, -1, keepdims=True)
        inv = lax.rsqrt(total + epsilon)
        near = near * inv
        txt_emb[r : r + block, 0:two] = near.astype(BF)
        txt_emb[r : r + block, two:] = (far * inv).astype(BF)
        txt_own_t[:, r : r + block] = jnp.transpose(near[:, 0:256])[0:cols, :].astype(BF)
    for n, r in enumerate(range(0, pairs, block)):
        at = slice(r, r + block)
        loads[8 + 2 * n].wait()
        loads[9 + 2 * n].wait()
        far = dot(wi_s[...], img_s[at, :], NT)
        near = img_raw[:, at]
        total = jnp.sum(near * near, 0, keepdims=True) + jnp.sum(far * far, 0, keepdims=True)
        inv = lax.rsqrt(total + epsilon)
        near = near * inv
        img_emb_t[0:two, at] = near.astype(BF)
        img_emb_t[two:, at] = (far * inv).astype(BF)
        img_own_t[:, at] = near[0:cols, :]
        inv_ref[:, at] = inv
    saves = [
        pltpu.make_async_copy(img_emb_t, img_emb_hbm, out_sems.at[1]),
        pltpu.make_async_copy(img_own_t, img_own_hbm, out_sems.at[2]),
    ]
    for c in saves:
        c.start()

    def finish(at, img_part, along):
        img_part_ref[:, at] = img_part
        along_ref[:, at] = along

    score_tile(txt_emb, txt_own_t, img_emb_t, er_ref, ec_s, label_ref, g_s, finish)
    text_part(g_s, img_emb_t, cols, txt_part_ref)
    save_wt.wait()
    for c in saves:
        c.wait()


def project_texts(feats_ref, wt_ref, emb_ref, own_t_ref):
    cols = own_t_ref.shape[0]
    for r in range(0, emb_ref.shape[0], 512):
        raw = dot(feats_ref[r : r + 512, :], wt_ref[...], NT)
        unit = raw * lax.rsqrt(jnp.sum(raw * raw, -1, keepdims=True) + epsilon)
        emb_ref[r : r + 512, :] = unit.astype(BF)
        own_t_ref[:, r : r + 512] = jnp.transpose(unit[:, 0:256])[0:cols, :].astype(BF)


def stand_half(feats, place, lse_s, ec_s):
    half = ec_s.shape[0]
    parts = [feats[half:, n * 128 : (n + 1) * 128].astype(F32) for n in range(3)]
    lse_s[...] = (parts[0] + parts[1]) + parts[2]
    stand(lse_s, place * (half // 128), ec_s)


def second_kernel(
    feats, wt, img_emb_hbm, er_ref, img_part_hbm, along_in,
    img_part_ref, along_ref, txt_part_ref,
    img_emb_t, img_part_s, txt_emb, txt_own_t, lse_s, ec_s, g_s, sems,
):
    loads = copies([(img_emb_hbm, img_emb_t), (img_part_hbm, img_part_s)], sems)
    stand_half(feats, lax.axis_index("core"), lse_s, ec_s)
    project_texts(feats, wt, txt_emb, txt_own_t)
    loads[0].wait()

    def finish(at, img_part, along):
        if at.start == 0:
            loads[1].wait()
        img_part_ref[:, at] = img_part_s[:, at] + img_part
        along_ref[:, at] = along_in[:, at] + along

    score_tile(txt_emb, txt_own_t, img_emb_t, er_ref, ec_s, None, g_s, finish)
    text_part(g_s, img_emb_t, txt_own_t.shape[0], txt_part_ref)


def last_kernel(
    feats, wt, img_emb_hbm, er_ref, img_part_hbm, along_in, img_own_hbm, inv_ref, img_hbm,
    pieces_ref, txt_part_ref,
    img_emb_t, img_part_s, img_own_t, img_s, txt_emb, txt_own_t, lse_s, ec_s, g_s, d_raw, sems,
):
    loads = copies(
        [
            (img_emb_hbm, img_emb_t), (img_part_hbm, img_part_s),
            (img_own_hbm, img_own_t), (img_hbm, img_s),
        ],
        sems,
    )
    stand_half(feats, 1 - lax.axis_index("core"), lse_s, ec_s)
    project_texts(feats, wt, txt_emb, txt_own_t)
    loads[0].wait()

    def finish(at, img_part, along):
        if at.start == 0:
            loads[1].wait()
            loads[2].wait()
        grad = img_part_s[:, at] + img_part
        toward = along_in[:, at] + along
        d_raw[:, at] = (
            (grad - img_own_t[:, at] * toward) * (scale_logit * inv_ref[:, at])
        ).astype(BF)

    score_tile(txt_emb, txt_own_t, img_emb_t, er_ref, ec_s, None, g_s, finish)
    loads[3].wait()
    n_pieces, rb, cb = pieces_ref.shape
    across = img_s.shape[1] // cb
    for k in range(0, img_s.shape[1], 256):
        part = dot(d_raw[...], img_s[:, k : k + 256], NN)
        for r in range(n_pieces // across):
            for c in range(256 // cb):
                pieces_ref[r * across + k // cb + c] = part[
                    r * rb : (r + 1) * rb, c * cb : (c + 1) * cb
                ].astype(BF)
    text_part(g_s, img_emb_t, txt_own_t.shape[0], txt_part_ref)


def text_total_kernel(part_a, part_b, carry, out_ref):
    half = part_a.shape[1]
    core = lax.axis_index("core")
    for place, part in ((core, part_a), (1 - core, part_b)):
        at = pl.ds(pl.multiple_of(place * half, half), half)
        out_ref[:, at] = part[...] + carry[:, at].astype(F32)


def local(sizes, img_feats, txt_feats, img_weight, txt_weight, row_lse, col_lse, labels):
    n_yl, n_x, n_z, n_yh, n_core = sizes
    n_dp = n_yl * n_x * n_z
    pairs = img_feats.shape[0]
    cols = img_weight.shape[1]
    width = cols * n_yh * n_core
    img_in, txt_in = img_feats.shape[1], txt_feats.shape[1]
    core = lax.axis_index("core")
    yh = lax.axis_index("yh")

    across = routes(sizes, lambda yl, x, z, h, c: (1 - yl, x, z, 1 - h, c))
    swap = routes(sizes, lambda yl, x, z, h, c: (yl, x, z, h, 1 - c))
    peer = routes(sizes, lambda yl, x, z, h, c: (yl, x, z, 1 - h, c))

    cross = routes(sizes, lambda yl, x, z, h, c: (yl, x, z, 1 - h, 1 - c))

    def following(yl, x, z, h, c):
        d = ((yl * n_x + x) * n_z + z + 1) % n_dp
        return (d // (n_x * n_z), (d // n_z) % n_x, d % n_z, h, c)

    onward = routes(sizes, following)

    def send(a, route):
        return lax.ppermute(a, AXES, route)

    def ordered(bit, own, other):
        first = jnp.where(bit == 0, own, other)
        second = jnp.where(bit == 0, other, own)
        return jnp.concatenate([first, second], 1)

    shape = jax.ShapeDtypeStruct
    half = pairs // n_core
    lse = col_lse.reshape(pairs // 128, 128)
    parcel, w_own = call(
        parcel_kernel,
        [ANY, VMEM, ANY, ANY],
        [
            (shape((half + lse.shape[0], txt_in), BF), VMEM),
            (shape((cols, img_in + txt_in), BF), VMEM),
        ],
        [pltpu.SemaphoreType.DMA((3,))],
        0,
        0,
    )(txt_feats, lse, img_weight.T, txt_weight.T)
    feats_a = send(parcel, onward)
    w_far = send(w_own, across)
    w_near = send(w_own, swap)
    w_far_near = send(w_far, swap)
    img_raw, txt_raw, er_own = call(
        near_kernel,
        [ANY, ANY, VMEM, VMEM, VMEM],
        [
            (shape((2 * cols, pairs), F32), VMEM),
            (shape((pairs, 2 * cols), F32), VMEM),
            (shape((1, row_lse.shape[0]), F32), VMEM),
        ],
        [
            pltpu.VMEM((pairs, img_in), BF),
            pltpu.VMEM((pairs, txt_in), BF),
            pltpu.VMEM((2 * cols, img_in), BF),
            pltpu.VMEM((2 * cols, txt_in), BF),
            pltpu.SemaphoreType.DMA((8,)),
        ],
        2 * pairs * 2 * cols * (img_in + txt_in),
        2 * pairs * (img_in + txt_in + 2 * width),
    )(img_feats, txt_feats, w_own, w_near, row_lse[None, :])
    er_near = send(er_own, swap)
    er_far = send(er_own, peer)
    er_far_near = send(er_own, cross)
    er = ordered(yh, ordered(core, er_own, er_near), ordered(core, er_far, er_far_near))

    tile_flops = 2 * pairs * pairs * (width + 2 * cols)
    img_emb_t, img_own_t, wt, inv, img_part, along, txt_part = call(
        first_kernel,
        [ANY] * 4 + [VMEM] * 7,
        [
            (shape((width, pairs), BF), ANY),
            (shape((cols, pairs), F32), ANY),
            (shape((width, txt_in), BF), ANY),
            (shape((1, pairs), F32), VMEM),
            (shape((cols, pairs), F32), VMEM),
            (shape((1, pairs), F32), VMEM),
            (shape((cols, pairs), BF), VMEM),
        ],
        [
            pltpu.VMEM((pairs, txt_in), BF),
            pltpu.VMEM((pairs, 2 * cols), F32),
            pltpu.VMEM((pairs, img_in), BF),
            pltpu.VMEM((2 * cols, pairs), F32),
            pltpu.VMEM((2 * cols, img_in), BF),
            pltpu.VMEM((width, txt_in), BF),
            pltpu.VMEM((pairs, width), BF),
            pltpu.VMEM((cols, pairs), BF),
            pltpu.VMEM((width, pairs), BF),
            pltpu.VMEM((cols, pairs), F32),
            pltpu.VMEM((pairs, 128), F32),
            pltpu.VMEM((pairs, pairs), BF),
            pltpu.SemaphoreType.DMA((16,)),
            pltpu.SemaphoreType.DMA((3,)),
        ],
        tile_flops,
        4 * pairs * width * 2,
        pairs * pairs,
    )(
        txt_feats, txt_raw, img_feats, img_raw, w_own, w_near, w_far, w_far_near, er, lse, labels
    )
    txt_carry = send(txt_part, onward)
    feats_a, along = lax.optimization_barrier((feats_a, along))
    feats_b = send(feats_a, swap)

    half_scratch = [
        pltpu.VMEM((half, width), BF),
        pltpu.VMEM((cols, half), BF),
        pltpu.VMEM((pairs // 128, 128), F32),
        pltpu.VMEM((half, 128), F32),
        pltpu.VMEM((half, pairs), BF),
    ]
    img_part, along, txt_a = call(
        second_kernel,
        [VMEM, VMEM, ANY, VMEM, ANY, VMEM],
        [
            (shape((cols, pairs), F32), VMEM),
            (shape((1, pairs), F32), VMEM),
            (shape((cols, half), F32), VMEM),
        ],
        [pltpu.VMEM((width, pairs), BF), pltpu.VMEM((cols, pairs), F32)]
        + half_scratch
        + [pltpu.SemaphoreType.DMA((2,))],
        tile_flops // 2,
        2 * pairs * width * 2,
        pairs * half,
    )(feats_a, wt, img_emb_t, er, img_part, along)
    pieces, txt_b = call(
        last_kernel,
        [VMEM, VMEM, ANY, VMEM, ANY, VMEM, ANY, VMEM, ANY],
        [(shape((n_dp, cols * img_in // (128 * n_dp), 128), BF), VMEM), (shape((cols, half), F32), VMEM)],
        [
            pltpu.VMEM((width, pairs), BF),
            pltpu.VMEM((cols, pairs), F32),
            pltpu.VMEM((cols, pairs), F32),
            pltpu.VMEM((pairs, img_in), BF),
        ]
        + half_scratch
        + [pltpu.VMEM((cols, pairs), BF), pltpu.SemaphoreType.DMA((4,))],
        tile_flops // 2,
        2 * pairs * width * 2,
        pairs * half,
    )(feats_b, wt, img_emb_t, er, img_part, along, img_own_t, inv, img_feats)

    pieces, txt_carry = lax.optimization_barrier((pieces, txt_carry))
    got = lax.all_to_all(pieces, DP, 0, 0, tiled=True)
    total = jnp.sum(got.astype(F32), 0).astype(BF)
    spread = jnp.broadcast_to(total[None], pieces.shape)
    back = lax.all_to_all(spread, DP, 0, 0, tiled=True)
    (txt_total,) = call(
        text_total_kernel,
        [VMEM] * 3,
        [(shape((cols, pairs), F32), VMEM)],
        [],
        0,
        10 * cols * pairs,
    )(txt_a, txt_b, txt_carry)
    across_pieces = img_in // 128
    tiles = back.reshape(n_dp // across_pieces, across_pieces, pieces.shape[1], 128)
    weight_total = tiles.transpose(0, 2, 1, 3).reshape(cols, img_in).astype(F32)
    return weight_total.T, txt_total.T


def solution(mesh):
    n_dp, n_mp = mesh.devices.shape
    sizes = (2, 4, n_dp // 8, 2, n_mp // 2)
    fine = Mesh(mesh.devices.reshape(sizes), AXES)
    placed = (
        P(DP, None),
        P(DP, None),
        P(None, MP),
        P(None, MP),
        P(DP + MP),
        P(DP),
        P(DP, None),
    )
    return jax.shard_map(
        functools.partial(local, sizes),
        mesh=fine,
        in_specs=placed,
        out_specs=(P(None, MP), P(DP, MP)),
        check_vma=False,
    )
```

```python
import functools
import math

import jax
import jax.numpy as jnp
from jax import lax
from jax.experimental import pallas as pl
from jax.experimental.pallas import tpu as pltpu
from jax.sharding import Mesh, PartitionSpec as P

scale_logit = 1.0 / 0.07
loss_weight = 0.25
epsilon = 1e-06
exp_scale = scale_logit * math.log2(math.e)

AXES = ("yl", "x", "z", "yh", "core")
DP = ("yl", "x", "z")
MP = ("yh", "core")
BF = jnp.bfloat16
F32 = jnp.float32
VMEM_LIMIT = 56 * 1024 * 1024
TXT_CHUNK, IMG_CHUNK = 512, 256

NT = (((1,), (1,)), ((), ()))
NN = (((1,), (0,)), ((), ()))


def dot(a, b, dims):
    return lax.dot_general(a, b, dims, preferred_element_type=F32)


def routes(sizes, move):
    n_yl, n_x, n_z, n_yh, n_core = sizes

    def flat(p):
        yl, x, z, yh, core = p
        return (((yl * n_x + x) * n_z + z) * n_yh + yh) * n_core + core

    pairs = []
    for yl in range(n_yl):
        for x in range(n_x):
            for z in range(n_z):
                for yh in range(n_yh):
                    for core in range(n_core):
                        p = (yl, x, z, yh, core)
                        pairs.append((flat(p), flat(move(*p))))
    return pairs


VMEM = pl.BlockSpec(memory_space=pltpu.VMEM)
ANY = pl.BlockSpec(memory_space=pl.ANY)


def call(body, ins, outs, scratch, flops, bytes_accessed, transcendentals=0):
    return pl.pallas_call(
        body,
        out_shape=[shape for shape, _ in outs],
        in_specs=ins,
        out_specs=[spec for _, spec in outs],
        scratch_shapes=scratch,
        compiler_params=pltpu.CompilerParams(vmem_limit_bytes=VMEM_LIMIT),
        cost_estimate=pl.CostEstimate(
            flops=0, bytes_accessed=0, transcendentals=0
        ),
    )


def copies(pairs, sems):
    made = [pltpu.make_async_copy(a, b, sems.at[n]) for n, (a, b) in enumerate(pairs)]
    for c in made:
        c.start()
    return made


def parcel_kernel(txt_hbm, lse_ref, wi_hbm, wt_hbm, out_ref, w_ref, sems):
    rows = out_ref.shape[0] - lse_ref.shape[0]
    depth = wi_hbm.shape[1]
    first = pl.multiple_of(lax.axis_index("core") * rows, rows)
    loads = copies(
        [
            (wi_hbm, w_ref.at[:, pl.ds(0, depth)]),
            (wt_hbm, w_ref.at[:, pl.ds(depth, wt_hbm.shape[1])]),
        ]
        + [
            (txt_hbm.at[pl.ds(first + r, rows // 8), :], out_ref.at[pl.ds(r, rows // 8), :])
            for r in range(0, rows, rows // 8)
        ],
        sems,
    )
    lse = lse_ref[...]
    high = lse.astype(BF)
    rest = lse - high.astype(F32)
    middle = rest.astype(BF)
    low = (rest - middle.astype(F32)).astype(BF)
    for n, part in enumerate((high, middle, low)):
        out_ref[rows:, n * 128 : (n + 1) * 128] = part
    out_ref[rows:, 384:] = jnp.zeros((lse.shape[0], out_ref.shape[1] - 384), BF)
    for c in loads:
        c.wait()


def row_blocks(pairs):
    return [pl.ds(r, pairs // 4) for r in range(0, pairs, pairs // 4)]


def near_kernel(
    img_hbm, txt_hbm, w0, w1, row_ref,
    img_raw, txt_raw, er_ref,
    img_s, txt_s, wi_s, wt_s, sems,
):
    pairs, depth = img_s.shape
    block = pairs // 4
    blocks = row_blocks(pairs)
    loads = copies(
        [(txt_hbm.at[b, :], txt_s.at[b, :]) for b in blocks]
        + [(img_hbm.at[b, :], img_s.at[b, :]) for b in blocks],
        sems,
    )
    er_ref[...] = loss_weight * jnp.exp(-row_ref[...])
    cols = w0.shape[0]
    for n, w in enumerate((w0, w1)):
        wi_s[n * cols : (n + 1) * cols, :] = w[:, 0:depth]
        wt_s[n * cols : (n + 1) * cols, :] = w[:, depth:]
    for n in range(4):
        at = slice(n * block, (n + 1) * block)
        loads[n].wait()
        txt_raw[at, :] = dot(txt_s[at, :], wt_s[...], NT)
    for n in range(4):
        at = slice(n * block, (n + 1) * block)
        loads[4 + n].wait()
        img_raw[:, at] = dot(wi_s[...], img_s[at, :], NT)


def stand(lse_ref, first, column_ref):
    for n in range(column_ref.shape[0] // 128):
        weight = loss_weight * jnp.exp(-lse_ref[pl.ds(first + n, 1), :])
        column_ref[n * 128 : (n + 1) * 128, :] = jnp.transpose(jnp.broadcast_to(weight, (128, 128)))


def score_tile(txt_emb, txt_own_t, img_emb_t, er_ref, ec_s, label_ref, g_s, finish):
    texts = txt_emb.shape[0]
    for i in range(0, img_emb_t.shape[1], IMG_CHUNK):
        at = slice(i, i + IMG_CHUNK)
        along = jnp.zeros((1, IMG_CHUNK), F32)
        er = er_ref[:, at]
        for t in range(0, texts, TXT_CHUNK):
            raw = dot(txt_emb[t : t + TXT_CHUNK, :], img_emb_t[:, at], NN)
            g = jnp.exp2(raw * exp_scale) * (er + ec_s[t : t + TXT_CHUNK, 0:1])
            if label_ref is not None:
                place = lax.broadcasted_iota(jnp.int32, (TXT_CHUNK, IMG_CHUNK), 0)
                g = g - jnp.where(place == (label_ref[:, at] - t), 2.0 * loss_weight, 0.0)
            g = g.astype(BF)
            along = along + jnp.sum(g.astype(F32) * raw, 0, keepdims=True)
            g_s[t : t + TXT_CHUNK, at] = g
        finish(at, dot(txt_own_t[...], g_s[:, at], NN), along)


def text_part(g_s, img_emb_t, cols, out_ref):
    for t in range(0, g_s.shape[0], 256):
        out_ref[:, t : t + 256] = (
            scale_logit * dot(img_emb_t[0:cols, :], g_s[t : t + 256, :], NT)
        ).astype(out_ref.dtype)


def save_strip(src, dst, at, sems):
    lanes = pl.ds(at.start, IMG_CHUNK)
    c = pltpu.make_async_copy(src.at[:, lanes], dst.at[:, lanes], sems.at[at.start // IMG_CHUNK])
    c.start()
    return c


def first_kernel(
    txt_hbm, txt_raw_hbm, img_hbm, img_raw_hbm, w0, w1, w2, w3, er_ref, col_ref, label_ref,
    img_emb_hbm, img_own_hbm, wt_hbm, inv_ref, img_part_hbm, along_ref, txt_part_ref,
    txt_s, txt_raw, img_s, img_raw, wi_s, wt_s, txt_emb, txt_own_t, img_emb_t, img_own_t, ec_s, g_s,
    img_part_s, sems, out_sems, strip_sems,
):
    pairs = txt_s.shape[0]
    block = pairs // 4
    blocks = row_blocks(pairs)
    moves = []
    for b in blocks:
        moves += [(txt_hbm.at[b, :], txt_s.at[b, :]), (txt_raw_hbm.at[b, :], txt_raw.at[b, :])]
    for b in blocks:
        moves += [(img_hbm.at[b, :], img_s.at[b, :]), (img_raw_hbm.at[:, b], img_raw.at[:, b])]
    loads = copies(moves, sems)
    cols = w0.shape[0]
    depth = wi_s.shape[1]
    for n, w in enumerate((w0, w1, w2, w3)):
        wt_s[n * cols : (n + 1) * cols, :] = w[:, depth:]
    for n, w in enumerate((w2, w3)):
        wi_s[n * cols : (n + 1) * cols, :] = w[:, 0:depth]
    stand(col_ref, 0, ec_s)
    save_wt = pltpu.make_async_copy(wt_s, wt_hbm, out_sems.at[0])
    save_wt.start()
    two = 2 * cols
    for n, r in enumerate(range(0, pairs, block)):
        loads[2 * n].wait()
        loads[2 * n + 1].wait()
        far = dot(txt_s[r : r + block, :], wt_s[two:, :], NT)
        near = txt_raw[r : r + block, :]
        total = jnp.sum(near * near, -1, keepdims=True) + jnp.sum(far * far, -1, keepdims=True)
        inv = lax.rsqrt(total + epsilon)
        near = near * inv
        txt_emb[r : r + block, 0:two] = near.astype(BF)
        txt_emb[r : r + block, two:] = (far * inv).astype(BF)
        txt_own_t[:, r : r + block] = jnp.transpose(near[:, 0:256])[0:cols, :].astype(BF)
    for n, r in enumerate(range(0, pairs, block)):
        at = slice(r, r + block)
        loads[8 + 2 * n].wait()
        loads[9 + 2 * n].wait()
        far = dot(wi_s[...], img_s[at, :], NT)
        near = img_raw[:, at]
        total = jnp.sum(near * near, 0, keepdims=True) + jnp.sum(far * far, 0, keepdims=True)
        inv = lax.rsqrt(total + epsilon)
        near = near * inv
        img_emb_t[0:two, at] = near.astype(BF)
        img_emb_t[two:, at] = (far * inv).astype(BF)
        img_own_t[:, at] = near[0:cols, :]
        inv_ref[:, at] = inv
    saves = [
        pltpu.make_async_copy(img_emb_t, img_emb_hbm, out_sems.at[1]),
        pltpu.make_async_copy(img_own_t, img_own_hbm, out_sems.at[2]),
    ]
    for c in saves:
        c.start()

    def finish(at, img_part, along):
        img_part_s[:, at] = img_part
        along_ref[:, at] = along
        saves.append(save_strip(img_part_s, img_part_hbm, at, strip_sems))

    score_tile(txt_emb, txt_own_t, img_emb_t, er_ref, ec_s, label_ref, g_s, finish)
    text_part(g_s, img_emb_t, cols, txt_part_ref)
    save_wt.wait()
    for c in saves:
        c.wait()


def project_texts(feats_ref, wt_ref, emb_ref, own_t_ref):
    cols = own_t_ref.shape[0]
    for r in range(0, emb_ref.shape[0], 512):
        raw = dot(feats_ref[r : r + 512, :], wt_ref[...], NT)
        unit = raw * lax.rsqrt(jnp.sum(raw * raw, -1, keepdims=True) + epsilon)
        emb_ref[r : r + 512, :] = unit.astype(BF)
        own_t_ref[:, r : r + 512] = jnp.transpose(unit[:, 0:256])[0:cols, :].astype(BF)


def stand_half(feats, place, lse_s, ec_s):
    half = ec_s.shape[0]
    parts = [feats[half:, n * 128 : (n + 1) * 128].astype(F32) for n in range(3)]
    lse_s[...] = (parts[0] + parts[1]) + parts[2]
    stand(lse_s, place * (half // 128), ec_s)


def second_kernel(
    feats, wt, img_emb_hbm, er_ref, img_part_hbm, along_in,
    img_part_out, along_ref, g_hbm,
    img_emb_t, img_part_s, txt_emb, txt_own_t, lse_s, ec_s, g_s, sems, part_sems, g_sems,
):
    loads = copies([(img_emb_hbm, img_emb_t), (img_part_hbm, img_part_s)], sems)
    stand_half(feats, lax.axis_index("core"), lse_s, ec_s)
    project_texts(feats, wt, txt_emb, txt_own_t)
    loads[0].wait()

    saves = []

    def finish(at, img_part, along):
        if at.start == 0:
            loads[1].wait()
        img_part_s[:, at] = img_part_s[:, at] + img_part
        along_ref[:, at] = along_in[:, at] + along
        saves.append(save_strip(img_part_s, img_part_out, at, part_sems))
        saves.append(save_strip(g_s, g_hbm, at, g_sems))

    score_tile(txt_emb, txt_own_t, img_emb_t, er_ref, ec_s, None, g_s, finish)
    for c in saves:
        c.wait()


def last_kernel(
    feats, wt, img_emb_hbm, er_ref, img_part_hbm, along_in, img_own_hbm, inv_ref, img_hbm,
    pieces_ref, g_hbm,
    img_emb_t, img_part_s, img_own_t, img_s, txt_emb, txt_own_t, lse_s, ec_s, g_s, d_raw, sems, g_sems,
):
    loads = copies(
        [
            (img_emb_hbm, img_emb_t), (img_part_hbm, img_part_s),
            (img_own_hbm, img_own_t), (img_hbm, img_s),
        ],
        sems,
    )
    stand_half(feats, 1 - lax.axis_index("core"), lse_s, ec_s)
    project_texts(feats, wt, txt_emb, txt_own_t)
    loads[0].wait()

    saves = []

    def finish(at, img_part, along):
        if at.start == 0:
            loads[1].wait()
            loads[2].wait()
        grad = img_part_s[:, at] + img_part
        toward = along_in[:, at] + along
        d_raw[:, at] = (
            (grad - img_own_t[:, at] * toward) * (scale_logit * inv_ref[:, at])
        ).astype(BF)
        saves.append(save_strip(g_s, g_hbm, at, g_sems))

    score_tile(txt_emb, txt_own_t, img_emb_t, er_ref, ec_s, None, g_s, finish)
    loads[3].wait()
    n_pieces, rb, cb = pieces_ref.shape
    across = img_s.shape[1] // cb
    for k in range(0, img_s.shape[1], 256):
        part = dot(d_raw[...], img_s[:, k : k + 256], NN)
        for r in range(n_pieces // across):
            for c in range(256 // cb):
                pieces_ref[r * across + k // cb + c] = part[
                    r * rb : (r + 1) * rb, c * cb : (c + 1) * cb
                ].astype(BF)
    for c in saves:
        c.wait()


def text_total_kernel(g_a, g_b, img_emb_hbm, carry, out_ref, own_s, g_s, own_sem, sems):
    half = g_a.shape[0]
    block = half // 4
    core = lax.axis_index("core")
    own = pltpu.make_async_copy(img_emb_hbm.at[pl.ds(0, own_s.shape[0]), :], own_s, own_sem)
    own.start()
    moves = [
        (g.at[pl.ds(r, block), :], g_s.at[pl.ds(n * half + r, block), :])
        for n, g in enumerate((g_a, g_b))
        for r in range(0, half, block)
    ]
    loads = copies(moves, sems)
    own.wait()
    for n, place in enumerate((core, 1 - core)):
        for m in range(4):
            loads[4 * n + m].wait()
            r = n * half + m * block
            part = scale_logit * dot(own_s[...], g_s[r : r + block, :], NT)
            at = pl.ds(pl.multiple_of(place * half + m * block, block), block)
            out_ref[:, at] = part + carry[:, at].astype(F32)


def local(sizes, img_feats, txt_feats, img_weight, txt_weight, row_lse, col_lse, labels):
    n_yl, n_x, n_z, n_yh, n_core = sizes
    n_dp = n_yl * n_x * n_z
    pairs = img_feats.shape[0]
    cols = img_weight.shape[1]
    width = cols * n_yh * n_core
    img_in, txt_in = img_feats.shape[1], txt_feats.shape[1]
    core = lax.axis_index("core")
    yh = lax.axis_index("yh")

    across = routes(sizes, lambda yl, x, z, h, c: (1 - yl, x, z, 1 - h, c))
    swap = routes(sizes, lambda yl, x, z, h, c: (yl, x, z, h, 1 - c))
    peer = routes(sizes, lambda yl, x, z, h, c: (yl, x, z, 1 - h, c))

    cross = routes(sizes, lambda yl, x, z, h, c: (yl, x, z, 1 - h, 1 - c))

    def following(yl, x, z, h, c):
        d = ((yl * n_x + x) * n_z + z + 1) % n_dp
        return (d // (n_x * n_z), (d // n_z) % n_x, d % n_z, h, c)

    onward = routes(sizes, following)

    def send(a, route):
        return lax.ppermute(a, AXES, route)

    def ordered(bit, own, other):
        first = jnp.where(bit == 0, own, other)
        second = jnp.where(bit == 0, other, own)
        return jnp.concatenate([first, second], 1)

    shape = jax.ShapeDtypeStruct
    half = pairs // n_core
    lse = col_lse.reshape(pairs // 128, 128)
    parcel, w_own = call(
        parcel_kernel,
        [ANY, VMEM, ANY, ANY],
        [
            (shape((half + lse.shape[0], txt_in), BF), VMEM),
            (shape((cols, img_in + txt_in), BF), VMEM),
        ],
        [pltpu.SemaphoreType.DMA((10,))],
        0,
        0,
    )(txt_feats, lse, img_weight.T, txt_weight.T)
    feats_a = send(parcel, onward)
    w_far = send(w_own, across)
    w_near = send(w_own, swap)
    w_far_near = send(w_far, swap)
    img_raw, txt_raw, er_own = call(
        near_kernel,
        [ANY, ANY, VMEM, VMEM, VMEM],
        [
            (shape((2 * cols, pairs), F32), VMEM),
            (shape((pairs, 2 * cols), F32), VMEM),
            (shape((1, row_lse.shape[0]), F32), VMEM),
        ],
        [
            pltpu.VMEM((pairs, img_in), BF),
            pltpu.VMEM((pairs, txt_in), BF),
            pltpu.VMEM((2 * cols, img_in), BF),
            pltpu.VMEM((2 * cols, txt_in), BF),
            pltpu.SemaphoreType.DMA((8,)),
        ],
        2 * pairs * 2 * cols * (img_in + txt_in),
        2 * pairs * (img_in + txt_in + 2 * width),
    )(img_feats, txt_feats, w_own, w_near, row_lse[None, :])
    er_near = send(er_own, swap)
    er_far = send(er_own, peer)
    er_far_near = send(er_own, cross)
    er = ordered(yh, ordered(core, er_own, er_near), ordered(core, er_far, er_far_near))

    tile_flops = 2 * pairs * pairs * (width + 2 * cols)
    img_emb_t, img_own_t, wt, inv, img_part, along, txt_part = call(
        first_kernel,
        [ANY] * 4 + [VMEM] * 7,
        [
            (shape((width, pairs), BF), ANY),
            (shape((cols, pairs), F32), ANY),
            (shape((width, txt_in), BF), ANY),
            (shape((1, pairs), F32), VMEM),
            (shape((cols, pairs), F32), ANY),
            (shape((1, pairs), F32), VMEM),
            (shape((cols, pairs), BF), VMEM),
        ],
        [
            pltpu.VMEM((pairs, txt_in), BF),
            pltpu.VMEM((pairs, 2 * cols), F32),
            pltpu.VMEM((pairs, img_in), BF),
            pltpu.VMEM((2 * cols, pairs), F32),
            pltpu.VMEM((2 * cols, img_in), BF),
            pltpu.VMEM((width, txt_in), BF),
            pltpu.VMEM((pairs, width), BF),
            pltpu.VMEM((cols, pairs), BF),
            pltpu.VMEM((width, pairs), BF),
            pltpu.VMEM((cols, pairs), F32),
            pltpu.VMEM((pairs, 128), F32),
            pltpu.VMEM((pairs, pairs), BF),
            pltpu.VMEM((cols, pairs), F32),
            pltpu.SemaphoreType.DMA((16,)),
            pltpu.SemaphoreType.DMA((3,)),
            pltpu.SemaphoreType.DMA((pairs // IMG_CHUNK,)),
        ],
        tile_flops,
        4 * pairs * width * 2,
        pairs * pairs,
    )(
        txt_feats, txt_raw, img_feats, img_raw, w_own, w_near, w_far, w_far_near, er, lse, labels
    )
    txt_carry = send(txt_part, onward)
    feats_a, along = lax.optimization_barrier((feats_a, along))
    feats_b = send(feats_a, swap)

    strip_sems = [pltpu.SemaphoreType.DMA((pairs // IMG_CHUNK,))]
    half_scratch = [
        pltpu.VMEM((half, width), BF),
        pltpu.VMEM((cols, half), BF),
        pltpu.VMEM((pairs // 128, 128), F32),
        pltpu.VMEM((half, 128), F32),
        pltpu.VMEM((half, pairs), BF),
    ]
    img_part, along, g_a = call(
        second_kernel,
        [VMEM, VMEM, ANY, VMEM, ANY, VMEM],
        [
            (shape((cols, pairs), F32), ANY),
            (shape((1, pairs), F32), VMEM),
            (shape((half, pairs), BF), ANY),
        ],
        [pltpu.VMEM((width, pairs), BF), pltpu.VMEM((cols, pairs), F32)]
        + half_scratch
        + [pltpu.SemaphoreType.DMA((2,))] + strip_sems * 2,
        tile_flops // 2,
        2 * pairs * width * 2,
        pairs * half,
    )(feats_a, wt, img_emb_t, er, img_part, along)
    pieces, g_b = call(
        last_kernel,
        [VMEM, VMEM, ANY, VMEM, ANY, VMEM, ANY, VMEM, ANY],
        [(shape((n_dp, cols * img_in // (128 * n_dp), 128), BF), VMEM), (shape((half, pairs), BF), ANY)],
        [
            pltpu.VMEM((width, pairs), BF),
            pltpu.VMEM((cols, pairs), F32),
            pltpu.VMEM((cols, pairs), F32),
            pltpu.VMEM((pairs, img_in), BF),
        ]
        + half_scratch
        + [pltpu.VMEM((cols, pairs), BF), pltpu.SemaphoreType.DMA((4,))] + strip_sems,
        tile_flops // 2,
        2 * pairs * width * 2,
        pairs * half,
    )(feats_b, wt, img_emb_t, er, img_part, along, img_own_t, inv, img_feats)

    pieces, txt_carry = lax.optimization_barrier((pieces, txt_carry))
    got = lax.all_to_all(pieces, DP, 0, 0, tiled=True)
    total = jnp.sum(got.astype(F32), 0).astype(BF)
    spread = jnp.broadcast_to(total[None], pieces.shape)
    back = lax.all_to_all(spread, DP, 0, 0, tiled=True)
    (txt_total,) = call(
        text_total_kernel,
        [ANY, ANY, ANY, VMEM],
        [(shape((cols, pairs), F32), VMEM)],
        [
            pltpu.VMEM((cols, pairs), BF),
            pltpu.VMEM((pairs, pairs), BF),
            pltpu.SemaphoreType.DMA,
            pltpu.SemaphoreType.DMA((8,)),
        ],
        0,
        10 * cols * pairs,
    )(g_a, g_b, img_emb_t, txt_carry)
    across_pieces = img_in // 128
    tiles = back.reshape(n_dp // across_pieces, across_pieces, pieces.shape[1], 128)
    weight_total = tiles.transpose(0, 2, 1, 3).reshape(cols, img_in).astype(F32)
    return weight_total.T, txt_total.T


def solution(mesh):
    n_dp, n_mp = mesh.devices.shape
    sizes = (2, 4, n_dp // 8, 2, n_mp // 2)
    fine = Mesh(mesh.devices.reshape(sizes), AXES)
    placed = (
        P(DP, None),
        P(DP, None),
        P(None, MP),
        P(None, MP),
        P(DP + MP),
        P(DP),
        P(DP, None),
    )
    return jax.shard_map(
        functools.partial(local, sizes),
        mesh=fine,
        in_specs=placed,
        out_specs=(P(None, MP), P(DP, MP)),
        check_vma=False,
    )
```

```python
import functools
import math

import jax
import jax.numpy as jnp
from jax import lax
from jax.experimental import pallas as pl
from jax.experimental.pallas import tpu as pltpu
from jax.sharding import Mesh, PartitionSpec as P

scale_logit = 1.0 / 0.07
loss_weight = 0.25
epsilon = 1e-06
exp_scale = scale_logit * math.log2(math.e)

AXES = ("yl", "x", "z", "yh", "core")
DP = ("yl", "x", "z")
MP = ("yh", "core")
BF = jnp.bfloat16
F32 = jnp.float32
VMEM_LIMIT = 56 * 1024 * 1024
LAST_LIMIT = 44 * 1024 * 1024
TXT_CHUNK, IMG_CHUNK = 512, 256

NT = (((1,), (1,)), ((), ()))
NN = (((1,), (0,)), ((), ()))


def dot(a, b, dims):
    return lax.dot_general(a, b, dims, preferred_element_type=F32)


def routes(sizes, move):
    n_yl, n_x, n_z, n_yh, n_core = sizes

    def flat(p):
        yl, x, z, yh, core = p
        return (((yl * n_x + x) * n_z + z) * n_yh + yh) * n_core + core

    pairs = []
    for yl in range(n_yl):
        for x in range(n_x):
            for z in range(n_z):
                for yh in range(n_yh):
                    for core in range(n_core):
                        p = (yl, x, z, yh, core)
                        pairs.append((flat(p), flat(move(*p))))
    return pairs


VMEM = pl.BlockSpec(memory_space=pltpu.VMEM)
ANY = pl.BlockSpec(memory_space=pl.ANY)


def call(body, ins, outs, scratch, flops, bytes_accessed, transcendentals=0):
    return pl.pallas_call(
        body,
        out_shape=[shape for shape, _ in outs],
        in_specs=ins,
        out_specs=[spec for _, spec in outs],
        scratch_shapes=scratch,
        compiler_params=pltpu.CompilerParams(
            vmem_limit_bytes=LAST_LIMIT if body is last_kernel else VMEM_LIMIT
        ),
        cost_estimate=pl.CostEstimate(
            flops=0, bytes_accessed=0, transcendentals=0
        ),
    )


def copies(pairs, sems):
    made = [pltpu.make_async_copy(a, b, sems.at[n]) for n, (a, b) in enumerate(pairs)]
    for c in made:
        c.start()
    return made


def parcel_kernel(txt_hbm, lse_ref, wi_hbm, wt_hbm, out_ref, w_ref, sems):
    rows = out_ref.shape[0] - lse_ref.shape[0]
    depth = wi_hbm.shape[1]
    first = pl.multiple_of(lax.axis_index("core") * rows, rows)
    loads = copies(
        [
            (wi_hbm, w_ref.at[:, pl.ds(0, depth)]),
            (wt_hbm, w_ref.at[:, pl.ds(depth, wt_hbm.shape[1])]),
        ]
        + [
            (txt_hbm.at[pl.ds(first + r, rows // 8), :], out_ref.at[pl.ds(r, rows // 8), :])
            for r in range(0, rows, rows // 8)
        ],
        sems,
    )
    lse = lse_ref[...]
    high = lse.astype(BF)
    rest = lse - high.astype(F32)
    middle = rest.astype(BF)
    low = (rest - middle.astype(F32)).astype(BF)
    for n, part in enumerate((high, middle, low)):
        out_ref[rows:, n * 128 : (n + 1) * 128] = part
    out_ref[rows:, 384:] = jnp.zeros((lse.shape[0], out_ref.shape[1] - 384), BF)
    for c in loads:
        c.wait()


def row_blocks(pairs):
    return [pl.ds(r, pairs // 4) for r in range(0, pairs, pairs // 4)]


def near_kernel(
    img_hbm, txt_hbm, w0, w1, row_ref,
    img_raw, txt_raw, er_ref,
    img_s, txt_s, wi_s, wt_s, sems,
):
    pairs, depth = img_s.shape
    block = pairs // 4
    blocks = row_blocks(pairs)
    loads = copies(
        [(txt_hbm.at[b, :], txt_s.at[b, :]) for b in blocks]
        + [(img_hbm.at[b, :], img_s.at[b, :]) for b in blocks],
        sems,
    )
    er_ref[...] = loss_weight * jnp.exp(-row_ref[...])
    cols = w0.shape[0]
    for n, w in enumerate((w0, w1)):
        wi_s[n * cols : (n + 1) * cols, :] = w[:, 0:depth]
        wt_s[n * cols : (n + 1) * cols, :] = w[:, depth:]
    for n in range(4):
        at = slice(n * block, (n + 1) * block)
        loads[n].wait()
        txt_raw[at, :] = dot(txt_s[at, :], wt_s[...], NT)
    for n in range(4):
        at = slice(n * block, (n + 1) * block)
        loads[4 + n].wait()
        img_raw[:, at] = dot(wi_s[...], img_s[at, :], NT)


def stand(lse_ref, first, column_ref):
    for n in range(column_ref.shape[0] // 128):
        weight = loss_weight * jnp.exp(-lse_ref[pl.ds(first + n, 1), :])
        column_ref[n * 128 : (n + 1) * 128, :] = jnp.transpose(jnp.broadcast_to(weight, (128, 128)))


def score_tile(txt_emb, txt_own_t, img_emb_t, er_ref, ec_s, label_ref, g_s, finish):
    texts = txt_emb.shape[0]
    steps = [
        (i, t) for i in range(0, img_emb_t.shape[1], IMG_CHUNK) for t in range(0, texts, TXT_CHUNK)
    ]

    def product(i, t):
        return dot(txt_emb[t : t + TXT_CHUNK, :], img_emb_t[:, i : i + IMG_CHUNK], NN)

    def close(at, along):
        finish(at, dot(txt_own_t[...], g_s[:, at], NN), along)

    raw = product(*steps[0])
    done = None
    for n, (i, t) in enumerate(steps):
        ahead = product(*steps[n + 1]) if n + 1 < len(steps) else None
        if done is not None:
            close(*done)
            done = None
        at = slice(i, i + IMG_CHUNK)
        if t == 0:
            along = jnp.zeros((1, IMG_CHUNK), F32)
        g = jnp.exp2(raw * exp_scale) * (er_ref[:, at] + ec_s[t : t + TXT_CHUNK, 0:1])
        if label_ref is not None:
            place = lax.broadcasted_iota(jnp.int32, (TXT_CHUNK, IMG_CHUNK), 0)
            g = g - jnp.where(place == (label_ref[:, at] - t), 2.0 * loss_weight, 0.0)
        g = g.astype(BF)
        along = along + jnp.sum(g.astype(F32) * raw, 0, keepdims=True)
        g_s[t : t + TXT_CHUNK, at] = g
        if t + TXT_CHUNK == texts:
            done = (at, along)
        raw = ahead
    close(*done)


def text_part(g_s, img_emb_t, cols, out_ref):
    for t in range(0, g_s.shape[0], 256):
        out_ref[:, t : t + 256] = (
            scale_logit * dot(img_emb_t[0:cols, :], g_s[t : t + 256, :], NT)
        ).astype(out_ref.dtype)


def save_strip(src, dst, at, sems):
    lanes = pl.ds(at.start, IMG_CHUNK)
    c = pltpu.make_async_copy(src.at[:, lanes], dst.at[:, lanes], sems.at[at.start // IMG_CHUNK])
    c.start()
    return c


def first_kernel(
    txt_hbm, txt_raw_hbm, img_hbm, img_raw_hbm, w0, w1, w2, w3, er_ref, col_ref, label_ref,
    img_emb_hbm, img_own_hbm, wt_hbm, inv_ref, img_part_hbm, along_ref, txt_part_ref,
    txt_s, txt_raw, img_s, img_raw, wi_s, wt_s, txt_emb, txt_own_t, img_emb_t, img_own_t, ec_s, g_s,
    img_part_s, sems, out_sems, strip_sems,
):
    pairs = txt_s.shape[0]
    block = pairs // 4
    blocks = row_blocks(pairs)
    moves = []
    for b in blocks:
        moves += [(txt_hbm.at[b, :], txt_s.at[b, :]), (txt_raw_hbm.at[b, :], txt_raw.at[b, :])]
    for b in blocks:
        moves += [(img_hbm.at[b, :], img_s.at[b, :]), (img_raw_hbm.at[:, b], img_raw.at[:, b])]
    loads = copies(moves, sems)
    cols = w0.shape[0]
    depth = wi_s.shape[1]
    for n, w in enumerate((w0, w1, w2, w3)):
        wt_s[n * cols : (n + 1) * cols, :] = w[:, depth:]
    for n, w in enumerate((w2, w3)):
        wi_s[n * cols : (n + 1) * cols, :] = w[:, 0:depth]
    stand(col_ref, 0, ec_s)
    save_wt = pltpu.make_async_copy(wt_s, wt_hbm, out_sems.at[0])
    save_wt.start()
    two = 2 * cols
    for n, r in enumerate(range(0, pairs, block)):
        loads[2 * n].wait()
        loads[2 * n + 1].wait()
        far = dot(txt_s[r : r + block, :], wt_s[two:, :], NT)
        near = txt_raw[r : r + block, :]
        total = jnp.sum(near * near, -1, keepdims=True) + jnp.sum(far * far, -1, keepdims=True)
        inv = lax.rsqrt(total + epsilon)
        near = near * inv
        txt_emb[r : r + block, 0:two] = near.astype(BF)
        txt_emb[r : r + block, two:] = (far * inv).astype(BF)
        txt_own_t[:, r : r + block] = jnp.transpose(near[:, 0:256])[0:cols, :].astype(BF)
    for n, r in enumerate(range(0, pairs, block)):
        at = slice(r, r + block)
        loads[8 + 2 * n].wait()
        loads[9 + 2 * n].wait()
        far = dot(wi_s[...], img_s[at, :], NT)
        near = img_raw[:, at]
        total = jnp.sum(near * near, 0, keepdims=True) + jnp.sum(far * far, 0, keepdims=True)
        inv = lax.rsqrt(total + epsilon)
        near = near * inv
        img_emb_t[0:two, at] = near.astype(BF)
        img_emb_t[two:, at] = (far * inv).astype(BF)
        img_own_t[:, at] = near[0:cols, :]
        inv_ref[:, at] = inv
    saves = [
        pltpu.make_async_copy(img_emb_t, img_emb_hbm, out_sems.at[1]),
        pltpu.make_async_copy(img_own_t, img_own_hbm, out_sems.at[2]),
    ]
    for c in saves:
        c.start()

    def finish(at, img_part, along):
        img_part_s[:, at] = img_part
        along_ref[:, at] = along
        saves.append(save_strip(img_part_s, img_part_hbm, at, strip_sems))

    score_tile(txt_emb, txt_own_t, img_emb_t, er_ref, ec_s, label_ref, g_s, finish)
    text_part(g_s, img_emb_t, cols, txt_part_ref)
    save_wt.wait()
    for c in saves:
        c.wait()


def project_texts(feats_ref, wt_ref, emb_ref, own_t_ref):
    cols = own_t_ref.shape[0]
    for r in range(0, emb_ref.shape[0], 512):
        raw = dot(feats_ref[r : r + 512, :], wt_ref[...], NT)
        unit = raw * lax.rsqrt(jnp.sum(raw * raw, -1, keepdims=True) + epsilon)
        emb_ref[r : r + 512, :] = unit.astype(BF)
        own_t_ref[:, r : r + 512] = jnp.transpose(unit[:, 0:256])[0:cols, :].astype(BF)


def stand_half(feats, place, lse_s, ec_s):
    half = ec_s.shape[0]
    parts = [feats[half:, n * 128 : (n + 1) * 128].astype(F32) for n in range(3)]
    lse_s[...] = (parts[0] + parts[1]) + parts[2]
    stand(lse_s, place * (half // 128), ec_s)


def second_kernel(
    feats, wt, img_emb_hbm, er_ref, img_part_hbm, along_in,
    img_part_out, along_ref, g_hbm,
    img_emb_t, img_part_s, txt_emb, txt_own_t, lse_s, ec_s, g_s, sems, part_sems, g_sems,
):
    loads = copies([(img_emb_hbm, img_emb_t), (img_part_hbm, img_part_s)], sems)
    stand_half(feats, lax.axis_index("core"), lse_s, ec_s)
    project_texts(feats, wt, txt_emb, txt_own_t)
    loads[0].wait()

    saves = []

    def finish(at, img_part, along):
        if at.start == 0:
            loads[1].wait()
        img_part_s[:, at] = img_part_s[:, at] + img_part
        along_ref[:, at] = along_in[:, at] + along
        saves.append(save_strip(img_part_s, img_part_out, at, part_sems))
        saves.append(save_strip(g_s, g_hbm, at, g_sems))

    score_tile(txt_emb, txt_own_t, img_emb_t, er_ref, ec_s, None, g_s, finish)
    for c in saves:
        c.wait()


def last_kernel(
    feats_any, wt, img_emb_hbm, er_ref, img_part_hbm, along_in, img_own_hbm, inv_ref, img_hbm,
    pieces_ref, g_hbm,
    feats, feats_sem, img_emb_t, img_part_s, img_own_t, img_s, txt_emb, txt_own_t, lse_s, ec_s, g_s, d_raw, sems, g_sems,
):
    texts = pltpu.make_async_copy(feats_any, feats, feats_sem)
    texts.start()
    loads = copies(
        [
            (img_emb_hbm, img_emb_t), (img_part_hbm, img_part_s),
            (img_own_hbm, img_own_t), (img_hbm, img_s),
        ],
        sems,
    )
    texts.wait()
    stand_half(feats, 1 - lax.axis_index("core"), lse_s, ec_s)
    project_texts(feats, wt, txt_emb, txt_own_t)
    loads[0].wait()

    saves = []

    def finish(at, img_part, along):
        if at.start == 0:
            loads[1].wait()
            loads[2].wait()
        grad = img_part_s[:, at] + img_part
        toward = along_in[:, at] + along
        d_raw[:, at] = (
            (grad - img_own_t[:, at] * toward) * (scale_logit * inv_ref[:, at])
        ).astype(BF)
        saves.append(save_strip(g_s, g_hbm, at, g_sems))

    score_tile(txt_emb, txt_own_t, img_emb_t, er_ref, ec_s, None, g_s, finish)
    loads[3].wait()
    n_pieces, rb, cb = pieces_ref.shape
    across = img_s.shape[1] // cb
    for k in range(0, img_s.shape[1], 256):
        part = dot(d_raw[...], img_s[:, k : k + 256], NN)
        for r in range(n_pieces // across):
            for c in range(256 // cb):
                pieces_ref[r * across + k // cb + c] = part[
                    r * rb : (r + 1) * rb, c * cb : (c + 1) * cb
                ].astype(BF)
    for c in saves:
        c.wait()


def text_total_kernel(g_a, g_b, img_emb_hbm, carry, out_ref, own_s, g_s, own_sem, sems):
    half = g_a.shape[0]
    block = half // 4
    core = lax.axis_index("core")
    own = pltpu.make_async_copy(img_emb_hbm.at[pl.ds(0, own_s.shape[0]), :], own_s, own_sem)
    own.start()
    moves = [
        (g.at[pl.ds(r, block), :], g_s.at[pl.ds(n * half + r, block), :])
        for n, g in enumerate((g_a, g_b))
        for r in range(0, half, block)
    ]
    loads = copies(moves, sems)
    own.wait()
    for n, place in enumerate((core, 1 - core)):
        for m in range(4):
            loads[4 * n + m].wait()
            r = n * half + m * block
            part = scale_logit * dot(own_s[...], g_s[r : r + block, :], NT)
            at = pl.ds(pl.multiple_of(place * half + m * block, block), block)
            out_ref[:, at] = part + carry[:, at].astype(F32)


def local(sizes, img_feats, txt_feats, img_weight, txt_weight, row_lse, col_lse, labels):
    n_yl, n_x, n_z, n_yh, n_core = sizes
    n_dp = n_yl * n_x * n_z
    pairs = img_feats.shape[0]
    cols = img_weight.shape[1]
    width = cols * n_yh * n_core
    img_in, txt_in = img_feats.shape[1], txt_feats.shape[1]
    core = lax.axis_index("core")
    yh = lax.axis_index("yh")

    across = routes(sizes, lambda yl, x, z, h, c: (1 - yl, x, z, 1 - h, c))
    swap = routes(sizes, lambda yl, x, z, h, c: (yl, x, z, h, 1 - c))
    peer = routes(sizes, lambda yl, x, z, h, c: (yl, x, z, 1 - h, c))

    cross = routes(sizes, lambda yl, x, z, h, c: (yl, x, z, 1 - h, 1 - c))

    def following(yl, x, z, h, c):
        d = ((yl * n_x + x) * n_z + z + 1) % n_dp
        return (d // (n_x * n_z), (d // n_z) % n_x, d % n_z, h, c)

    onward = routes(sizes, following)

    def send(a, route):
        return lax.ppermute(a, AXES, route)

    def ordered(bit, own, other):
        first = jnp.where(bit == 0, own, other)
        second = jnp.where(bit == 0, other, own)
        return jnp.concatenate([first, second], 1)

    shape = jax.ShapeDtypeStruct
    half = pairs // n_core
    lse = col_lse.reshape(pairs // 128, 128)
    parcel, w_own = call(
        parcel_kernel,
        [ANY, VMEM, ANY, ANY],
        [
            (shape((half + lse.shape[0], txt_in), BF), VMEM),
            (shape((cols, img_in + txt_in), BF), VMEM),
        ],
        [pltpu.SemaphoreType.DMA((10,))],
        0,
        0,
    )(txt_feats, lse, img_weight.T, txt_weight.T)
    feats_a = send(parcel, onward)
    w_far = send(w_own, across)
    w_near = send(w_own, swap)
    w_far_near = send(w_far, swap)
    img_raw, txt_raw, er_own = call(
        near_kernel,
        [ANY, ANY, VMEM, VMEM, VMEM],
        [
            (shape((2 * cols, pairs), F32), VMEM),
            (shape((pairs, 2 * cols), F32), VMEM),
            (shape((1, row_lse.shape[0]), F32), VMEM),
        ],
        [
            pltpu.VMEM((pairs, img_in), BF),
            pltpu.VMEM((pairs, txt_in), BF),
            pltpu.VMEM((2 * cols, img_in), BF),
            pltpu.VMEM((2 * cols, txt_in), BF),
            pltpu.SemaphoreType.DMA((8,)),
        ],
        2 * pairs * 2 * cols * (img_in + txt_in),
        2 * pairs * (img_in + txt_in + 2 * width),
    )(img_feats, txt_feats, w_own, w_near, row_lse[None, :])
    er_near = send(er_own, swap)
    er_far = send(er_own, peer)
    er_far_near = send(er_own, cross)
    er = ordered(yh, ordered(core, er_own, er_near), ordered(core, er_far, er_far_near))

    tile_flops = 2 * pairs * pairs * (width + 2 * cols)
    img_emb_t, img_own_t, wt, inv, img_part, along, txt_part = call(
        first_kernel,
        [ANY] * 4 + [VMEM] * 7,
        [
            (shape((width, pairs), BF), ANY),
            (shape((cols, pairs), F32), ANY),
            (shape((width, txt_in), BF), ANY),
            (shape((1, pairs), F32), VMEM),
            (shape((cols, pairs), F32), ANY),
            (shape((1, pairs), F32), VMEM),
            (shape((cols, pairs), BF), VMEM),
        ],
        [
            pltpu.VMEM((pairs, txt_in), BF),
            pltpu.VMEM((pairs, 2 * cols), F32),
            pltpu.VMEM((pairs, img_in), BF),
            pltpu.VMEM((2 * cols, pairs), F32),
            pltpu.VMEM((2 * cols, img_in), BF),
            pltpu.VMEM((width, txt_in), BF),
            pltpu.VMEM((pairs, width), BF),
            pltpu.VMEM((cols, pairs), BF),
            pltpu.VMEM((width, pairs), BF),
            pltpu.VMEM((cols, pairs), F32),
            pltpu.VMEM((pairs, 128), F32),
            pltpu.VMEM((pairs, pairs), BF),
            pltpu.VMEM((cols, pairs), F32),
            pltpu.SemaphoreType.DMA((16,)),
            pltpu.SemaphoreType.DMA((3,)),
            pltpu.SemaphoreType.DMA((pairs // IMG_CHUNK,)),
        ],
        tile_flops,
        4 * pairs * width * 2,
        pairs * pairs,
    )(
        txt_feats, txt_raw, img_feats, img_raw, w_own, w_near, w_far, w_far_near, er, lse, labels
    )
    txt_carry = send(txt_part, onward)
    feats_a, along = lax.optimization_barrier((feats_a, along))
    feats_b = send(feats_a, swap)

    strip_sems = [pltpu.SemaphoreType.DMA((pairs // IMG_CHUNK,))]
    half_scratch = [
        pltpu.VMEM((half, width), BF),
        pltpu.VMEM((cols, half), BF),
        pltpu.VMEM((pairs // 128, 128), F32),
        pltpu.VMEM((half, 128), F32),
        pltpu.VMEM((half, pairs), BF),
    ]
    img_part, along, g_a = call(
        second_kernel,
        [VMEM, VMEM, ANY, VMEM, ANY, VMEM],
        [
            (shape((cols, pairs), F32), ANY),
            (shape((1, pairs), F32), VMEM),
            (shape((half, pairs), BF), ANY),
        ],
        [pltpu.VMEM((width, pairs), BF), pltpu.VMEM((cols, pairs), F32)]
        + half_scratch
        + [pltpu.SemaphoreType.DMA((2,))] + strip_sems * 2,
        tile_flops // 2,
        2 * pairs * width * 2,
        pairs * half,
    )(feats_a, wt, img_emb_t, er, img_part, along)
    pieces, g_b = call(
        last_kernel,
        [ANY, VMEM, ANY, VMEM, ANY, VMEM, ANY, VMEM, ANY],
        [(shape((n_dp, cols * img_in // (128 * n_dp), 128), BF), VMEM), (shape((half, pairs), BF), ANY)],
        [
            pltpu.VMEM(parcel.shape, BF),
            pltpu.SemaphoreType.DMA,
            pltpu.VMEM((width, pairs), BF),
            pltpu.VMEM((cols, pairs), F32),
            pltpu.VMEM((cols, pairs), F32),
            pltpu.VMEM((pairs, img_in), BF),
        ]
        + half_scratch
        + [pltpu.VMEM((cols, pairs), BF), pltpu.SemaphoreType.DMA((4,))] + strip_sems,
        tile_flops // 2,
        2 * pairs * width * 2,
        pairs * half,
    )(feats_b, wt, img_emb_t, er, img_part, along, img_own_t, inv, img_feats)

    pieces, txt_carry = lax.optimization_barrier((pieces, txt_carry))
    got = lax.all_to_all(pieces, DP, 0, 0, tiled=True)
    total = jnp.sum(got.astype(F32), 0).astype(BF)
    spread = jnp.broadcast_to(total[None], pieces.shape)
    back = lax.all_to_all(spread, DP, 0, 0, tiled=True)
    (txt_total,) = call(
        text_total_kernel,
        [ANY, ANY, ANY, VMEM],
        [(shape((cols, pairs), F32), VMEM)],
        [
            pltpu.VMEM((cols, pairs), BF),
            pltpu.VMEM((pairs, pairs), BF),
            pltpu.SemaphoreType.DMA,
            pltpu.SemaphoreType.DMA((8,)),
        ],
        0,
        10 * cols * pairs,
    )(g_a, g_b, img_emb_t, txt_carry)
    across_pieces = img_in // 128
    tiles = back.reshape(n_dp // across_pieces, across_pieces, pieces.shape[1], 128)
    weight_total = tiles.transpose(0, 2, 1, 3).reshape(cols, img_in).astype(F32)
    return weight_total.T, txt_total.T


def solution(mesh):
    n_dp, n_mp = mesh.devices.shape
    sizes = (2, 4, n_dp // 8, 2, n_mp // 2)
    fine = Mesh(mesh.devices.reshape(sizes), AXES)
    placed = (
        P(DP, None),
        P(DP, None),
        P(None, MP),
        P(None, MP),
        P(DP + MP),
        P(DP),
        P(DP, None),
    )
    return jax.shard_map(
        functools.partial(local, sizes),
        mesh=fine,
        in_specs=placed,
        out_specs=(P(None, MP), P(DP, MP)),
        check_vma=False,
    )
```
